32 devices in a mesh: pool: 2 (over y), rep: 4 (over z), tp: 4 (over x, core).
Axes of the slice: x: 2, y: 2, z: 4, core: 2. Of those that a mesh axis runs over, the one named last changes fastest.
Arguments:
- hidden: bfloat16 [64, 8192], P(('pool', 'rep'), 'tp'), parts along dimension 0, may hold values from -6 to 6
- base_query_proj: bfloat16 [64, 8192], P(('pool', 'rep'), 'tp'), parts along dimension 0, may hold values from -10 to 10
- base_key_proj: bfloat16 [64, 1024], P(('pool', 'rep'), 'tp'), parts along dimension 0, may hold values from -6 to 6
- base_value_proj: bfloat16 [64, 1024], P(('pool', 'rep'), 'tp'), parts along dimension 0, may hold values from -6 to 6
- key_cache: bfloat16 [64, 512, 1024], P(('pool', 'rep'), None, 'tp'), parts along dimension 0, may hold values from -10 to 10
- value_cache: bfloat16 [64, 512, 1024], P(('pool', 'rep'), None, 'tp'), parts along dimension 0, may hold values from -6 to 6
- lengths: int32 [64], P('pool'), parts along dimension 0, may hold values from 2 to 511, as said below
- adapter_down_factors: bfloat16 [16, 8192, 192], P(('pool', 'rep'), 'tp'), parts along dimension 0, may hold values from -0.0625 to 0.0625
- adapter_up_query: bfloat16 [16, 64, 8192], P(('pool', 'rep'), None, 'tp'), parts along dimension 0, may hold values from -0.75 to 0.75
- adapter_up_key_value: bfloat16 [16, 2, 64, 1024], P(('pool', 'rep'), None, None, 'tp'), parts along dimension 0, may hold values from -0.75 to 0.75
- resident: int32 [8, 2], P('pool'), parts along dimension 0, may hold values from 0 to 63, as said below
- request_adapter_id: int32 [64], P(('pool', 'rep')), parts along dimension 0, may hold values from 0 to 63, as said below
- migration_offset: int32 [4], P('pool'), parts along dimension 0, may hold values from 1 to 3, as said below
Outputs:
- attended: bfloat16 [64, 8192], P(('pool', 'rep'), 'tp'), parts along dimension 0
- moved_keys: bfloat16 [16, 512, 1024], P(('pool', 'rep'), None, 'tp'), parts along dimension 0
- moved_values: bfloat16 [16, 512, 1024], P(('pool', 'rep'), None, 'tp'), parts along dimension 0
- arrived_down_factors: bfloat16 [16, 8192, 192], P(('pool', 'rep'), 'tp'), parts along dimension 0
- arrived_up_query: bfloat16 [16, 64, 8192], P(('pool', 'rep'), None, 'tp'), parts along dimension 0
- arrived_up_key_value: bfloat16 [16, 2, 64, 1024], P(('pool', 'rep'), None, None, 'tp'), parts along dimension 0
The draws below stay inside these ranges and needn't reach their ends.
There are 2 independent parts, one for each index of `pool`. The reference program is written for one: setup_inputs(seed, part) draws one part's arguments, and reference() takes and returns one part's arrays. A program takes and returns all parts, laid end to end along the dimension named above; each array names one. Nothing has to cross between parts.
Inputs may be any that keep to these rules, and one draw needn't show every extreme that they name: `lengths`: one request in every draw has exactly 511 cached positions. `resident`: the ids loaded on one replica all differ. `request_adapter_id`: every request's adapter is loaded on the replica that holds it on entry. `migration_offset`: all offsets differ.
All inputs are finite; a program needn't handle non-finite values.
Results may differ from the reference program's by a relative error of at most 0.0076.
Values may be sent and summed in bfloat16 or wider, within the bound.
No kernel may reach another device: no remote copies, remote signals or barrier semaphores. Data moves between devices by JAX's collectives and lax.ppermute only.
A program may use at most 64 MiB of HBM per device.

```python
import math
import jax
import jax.numpy as jnp
from jax import lax

MODEL_WIDTH = 8192
QUERY_HEADS = 64
KEY_VALUE_HEADS = 8
HEAD_SIZE = 128
ADAPTER_RANK = 64
RQ = 8
MIG = 2
CONTEXT_SLOTS = 512
NRES = 2
ADAPTERS = 64
REPLICAS = 4
REQUEST_TOTAL = 32
ADAPTER_POOL = 8


def adapter_tables(key):
    row_keys = jax.random.split(jax.random.fold_in(key, 201), REPLICAS)
    present_adapters = jax.vmap(lambda row_key: jax.random.permutation(row_key, ADAPTERS)[:NRES])(row_keys)
    slot_pick = jax.random.randint(jax.random.fold_in(key, 202), (REPLICAS, RQ), 0, NRES)
    requested = jnp.take_along_axis(present_adapters, slot_pick, axis=1).reshape(-1)
    return (present_adapters.astype(jnp.int32), requested.astype(jnp.int32))


def draw_base_query_proj(key, part):
    key = jax.random.fold_in(key, 11)
    value_rows = jax.random.truncated_normal(key, -6.0, 6.0, (REQUEST_TOTAL, QUERY_HEADS * HEAD_SIZE), jnp.float32)
    return value_rows.astype(jnp.bfloat16)


def draw_key_cache(key, part):
    key = jax.random.fold_in(key, 12)
    value_rows = jax.random.truncated_normal(key, -6.0, 6.0, (REQUEST_TOTAL, CONTEXT_SLOTS, KEY_VALUE_HEADS * HEAD_SIZE), jnp.float32)
    return value_rows.astype(jnp.bfloat16)


def draw_lengths(key, part):
    key = jax.random.fold_in(key, 13)
    ceilings = jax.random.randint(jax.random.fold_in(key, 1), (REPLICAS,), max(2, CONTEXT_SLOTS // 8), CONTEXT_SLOTS)
    drawn_lengths = jax.random.randint(jax.random.fold_in(key, 2), (REPLICAS, RQ), 2, ceilings[:, None] + 1)
    full_slot = jax.random.randint(jax.random.fold_in(key, 3), (), 0, REQUEST_TOTAL)
    flattened = drawn_lengths.reshape(-1)
    return jnp.where(jnp.arange(REQUEST_TOTAL) == full_slot, CONTEXT_SLOTS - 1, flattened).astype(jnp.int32)


def draw_resident(key, part):
    present_adapters, requested = adapter_tables(key)
    return present_adapters


def draw_request_adapter_id(key, part):
    present_adapters, requested = adapter_tables(key)
    return requested


def draw_migration_offset(key, part):
    key = jax.random.fold_in(key, 16)
    return (jax.random.permutation(key, REPLICAS - 1)[:MIG] + 1).astype(jnp.int32)


def shard_levels(own_key, shape, shards, smallest, high):
    level, own = 1.0, jax.random.fold_in(own_key, 6)
    for position, parts in shards:
        steps = jnp.exp(jax.random.uniform(jax.random.fold_in(own, position), (parts,), jnp.float32, smallest / len(shards), high / len(shards)))
        level = level * jnp.repeat(steps, shape[position] // parts).reshape([-1 if axis == position else 1 for axis in range(len(shape))])
    return level


def scatter_about(own_key, shape, deviation, most, cuts=(), kind=jnp.bfloat16):
    values = jax.random.normal(own_key, shape, jnp.float32) * deviation
    if len(cuts) > 0:
        values = shard_levels(own_key, shape, cuts, -0.22, 0.18) * values
    return jnp.clip(values, min=-most, max=most).astype(kind)


def setup_inputs(seed: int = 0, part: int = 0) -> dict:
    arg_keys = jax.random.split(jax.random.key(seed), 14)
    part_splits = jax.random.split(jax.random.fold_in(arg_keys[13], part), 14)
    return {
        "hidden": scatter_about(part_splits[0], (REQUEST_TOTAL, MODEL_WIDTH), 1.0, 6.0, ((0, 4), (1, 4))),
        "base_query_proj": draw_base_query_proj(jax.random.fold_in(jax.random.fold_in(arg_keys[13], part), 71), part),
        "base_key_proj": scatter_about(part_splits[2], (REQUEST_TOTAL, KEY_VALUE_HEADS * HEAD_SIZE), 1.0, 6.0, ((0, 4), (1, 4))),
        "base_value_proj": scatter_about(part_splits[3], (REQUEST_TOTAL, KEY_VALUE_HEADS * HEAD_SIZE), 1.0, 6.0, ((0, 4), (1, 4))),
        "key_cache": draw_key_cache(jax.random.fold_in(jax.random.fold_in(arg_keys[13], part), 71), part),
        "value_cache": scatter_about(part_splits[5], (REQUEST_TOTAL, CONTEXT_SLOTS, KEY_VALUE_HEADS * HEAD_SIZE), 1.0, 6.0, ((0, 4), (2, 4))),
        "lengths": draw_lengths(jax.random.fold_in(jax.random.fold_in(arg_keys[13], part), 71), part),
        "adapter_down_factors": scatter_about(part_splits[7], (ADAPTER_POOL, MODEL_WIDTH, 3 * ADAPTER_RANK), MODEL_WIDTH ** -0.5, 0.0625, ((0, 4), (1, 4))),
        "adapter_up_query": scatter_about(part_splits[8], (ADAPTER_POOL, ADAPTER_RANK, QUERY_HEADS * HEAD_SIZE), ADAPTER_RANK ** -0.5, 0.75, ((0, 4), (2, 4))),
        "adapter_up_key_value": scatter_about(part_splits[9], (ADAPTER_POOL, 2, ADAPTER_RANK, KEY_VALUE_HEADS * HEAD_SIZE), ADAPTER_RANK ** -0.5, 0.75, ((0, 4), (3, 4))),
        "resident": draw_resident(jax.random.fold_in(jax.random.fold_in(arg_keys[13], part), 71), part),
        "request_adapter_id": draw_request_adapter_id(jax.random.fold_in(jax.random.fold_in(arg_keys[13], part), 71), part),
        "migration_offset": draw_migration_offset(jax.random.fold_in(jax.random.fold_in(arg_keys[13], part), 71), part),
    }


def attend(query, keys, value_rows, key_new, value_new, lengths_now):
    batch_rows = query.shape[0]
    positions = keys.shape[1]
    kv_heads = key_new.shape[1] // HEAD_SIZE
    group_size = query.shape[1] // (kv_heads * HEAD_SIZE)
    factor = 1.0 / math.sqrt(HEAD_SIZE)
    q_heads = query.astype(jnp.float32).reshape(batch_rows, kv_heads, group_size, HEAD_SIZE)
    k_heads = keys.astype(jnp.float32).reshape(batch_rows, positions, kv_heads, HEAD_SIZE)
    v_heads = value_rows.astype(jnp.float32).reshape(batch_rows, positions, kv_heads, HEAD_SIZE)
    new_keys = key_new.astype(jnp.float32).reshape(batch_rows, kv_heads, HEAD_SIZE)
    new_values = value_new.astype(jnp.float32).reshape(batch_rows, kv_heads, HEAD_SIZE)
    scores = jnp.einsum('nhgd,nthd->nhgt', q_heads, k_heads) * factor
    fresh = jnp.einsum('nhgd,nhd->nhg', q_heads, new_keys) * factor
    valid = (jnp.arange(positions, dtype=jnp.int32)[None, :] < lengths_now[:, None])[:, None, None, :]
    peak = jnp.maximum(lax.optimization_barrier(jnp.max(jnp.where(valid, scores, -1e+30), axis=-1)), fresh)
    raised = jnp.where(valid, jnp.exp(scores - peak[..., None]), 0.0)
    raised_new = jnp.exp(fresh - peak)
    total = lax.optimization_barrier(jnp.sum(raised, axis=-1)) + raised_new
    weights = (raised / total[..., None]).astype(jnp.bfloat16)
    weight_new = (raised_new / total).astype(jnp.bfloat16)
    mixed = jnp.einsum('nhgt,nthd->nhgd', weights.astype(jnp.float32), v_heads)
    mixed = mixed + weight_new.astype(jnp.float32)[..., None] * new_values[:, :, None, :]
    return mixed.reshape(batch_rows, -1).astype(jnp.bfloat16)

def reference(hidden, base_query_proj, base_key_proj, base_value_proj, key_cache, value_cache, lengths, adapter_down_factors, adapter_up_query, adapter_up_key_value, resident, request_adapter_id, migration_offset):
    replicas = resident.shape[0]
    present_adapters = resident.shape[1]
    count_of_rows = hidden.shape[0] // replicas
    moving = migration_offset.shape[0]

    def replica_share(array, count):
        return array.reshape((replicas, count) + array.shape[1:])

    def single_replica(inputs):
        rows_x, rows_q, rows_k, rows_v, keys, value_rows, lengths_now, down, up_query, up_pair, res_row, ids = inputs
        indicator_matrix = (ids[:, None] == res_row[None, :]).astype(jnp.float32)
        every = jnp.einsum('wb,xbm->wxm', rows_x.astype(jnp.float32), down.astype(jnp.float32))
        shrunk = lax.optimization_barrier(jnp.sum(indicator_matrix[:, :, None] * every, axis=1)).astype(jnp.bfloat16)

        def expand(part, up_factor):
            every_up = jnp.einsum('rk,akc->rac', part.astype(jnp.float32), up_factor.astype(jnp.float32))
            return lax.optimization_barrier(jnp.sum(indicator_matrix[:, :, None] * every_up, axis=1))
        query = (rows_q.astype(jnp.float32) + expand(shrunk[:, :ADAPTER_RANK], up_query)).astype(jnp.bfloat16)
        key_new = (rows_k.astype(jnp.float32) + expand(shrunk[:, ADAPTER_RANK:2 * ADAPTER_RANK], up_pair[:, 0])).astype(jnp.bfloat16)
        value_new = (rows_v.astype(jnp.float32) + expand(shrunk[:, 2 * ADAPTER_RANK:], up_pair[:, 1])).astype(jnp.bfloat16)
        return (attend(query, keys, value_rows, key_new, value_new, lengths_now), key_new, value_new)
    completed, produced_keys, produced_values = lax.map(single_replica, (replica_share(hidden, count_of_rows), replica_share(base_query_proj, count_of_rows), replica_share(base_key_proj, count_of_rows), replica_share(base_value_proj, count_of_rows), replica_share(key_cache, count_of_rows), replica_share(value_cache, count_of_rows), replica_share(lengths, count_of_rows), replica_share(adapter_down_factors, present_adapters), replica_share(adapter_up_query, present_adapters), replica_share(adapter_up_key_value, present_adapters), resident, replica_share(request_adapter_id, count_of_rows)))
    remaining_requests = count_of_rows - moving
    slot_index = jnp.arange(count_of_rows, dtype=jnp.int32)
    shift_of = jnp.concatenate([jnp.zeros((remaining_requests,), jnp.int32), migration_offset.astype(jnp.int32)])
    source = (jnp.arange(replicas, dtype=jnp.int32)[:, None] - shift_of[None, :]) % replicas
    picked = completed[source, slot_index[None, :]]
    attended = picked.reshape(replicas * count_of_rows, -1)
    senders = (jnp.arange(replicas, dtype=jnp.int32)[:, None] - migration_offset.astype(jnp.int32)[None, :]) % replicas
    rows = (senders * count_of_rows + remaining_requests + jnp.arange(moving, dtype=jnp.int32)[None, :]).reshape(-1)
    sender_flat = senders.reshape(-1)
    new_keys = produced_keys.reshape(replicas * count_of_rows, -1)[rows]
    new_values = produced_values.reshape(replicas * count_of_rows, -1)[rows]
    spots = lengths[rows].astype(jnp.int32)
    place = (jnp.arange(key_cache.shape[1], dtype=jnp.int32)[None, :] == spots[:, None])[:, :, None]
    moved_keys = jnp.where(place, new_keys[:, None, :], key_cache[rows])
    moved_values = jnp.where(place, new_values[:, None, :], value_cache[rows])
    match = (resident[sender_flat] == request_adapter_id[rows][:, None]).astype(jnp.int32)
    slot = lax.optimization_barrier(jnp.sum(match * jnp.arange(present_adapters, dtype=jnp.int32)[None, :], axis=1))
    adapter_pool_rows = (sender_flat * present_adapters + slot).astype(jnp.int32)
    arrived_down_factors = adapter_down_factors[adapter_pool_rows]
    arrived_up_query = adapter_up_query[adapter_pool_rows]
    arrived_up_key_value = adapter_up_key_value[adapter_pool_rows]
    return (attended, moved_keys, moved_values, arrived_down_factors, arrived_up_query, arrived_up_key_value)
```

```python
import itertools
import math

import jax
import jax.numpy as jnp
from jax import lax
from jax.sharding import PartitionSpec as P

HEAD_SIZE = 128
MOST_JOINT_BRANCHES = 6


def shifted(shard, axis, by):
    size = lax.axis_size(axis)
    return lax.ppermute(shard, axis, [(i, (i + by) % size) for i in range(size)])


def attend(query, keys, value_rows, key_new, value_new, lengths_now):
    batch_rows = query.shape[0]
    positions = keys.shape[1]
    kv_heads = key_new.shape[1] // HEAD_SIZE
    group_size = query.shape[1] // (kv_heads * HEAD_SIZE)
    factor = 1.0 / math.sqrt(HEAD_SIZE)
    q_heads = query.reshape(batch_rows, kv_heads, group_size, HEAD_SIZE)
    k_heads = keys.reshape(batch_rows, positions, kv_heads, HEAD_SIZE)
    v_heads = value_rows.reshape(batch_rows, positions, kv_heads, HEAD_SIZE)
    new_keys = key_new.reshape(batch_rows, kv_heads, HEAD_SIZE)
    new_values = value_new.reshape(batch_rows, kv_heads, HEAD_SIZE).astype(jnp.float32)
    scores = (
        jnp.einsum("nhgd,nthd->nhgt", q_heads, k_heads, preferred_element_type=jnp.float32) * factor
    )
    fresh = (
        jnp.einsum("nhgd,nhd->nhg", q_heads, new_keys, preferred_element_type=jnp.float32) * factor
    )
    valid = (jnp.arange(positions, dtype=jnp.int32)[None, :] < lengths_now[:, None])[
        :, None, None, :
    ]
    peak = jnp.maximum(jnp.max(jnp.where(valid, scores, -1e30), axis=-1), fresh)
    raised = jnp.where(valid, jnp.exp(scores - peak[..., None]), 0.0)
    raised_new = jnp.exp(fresh - peak)
    total = jnp.sum(raised, axis=-1) + raised_new
    weights = (raised / total[..., None]).astype(jnp.bfloat16)
    weight_new = (raised_new / total).astype(jnp.bfloat16)
    mixed = jnp.einsum("nhgt,nthd->nhgd", weights, v_heads, preferred_element_type=jnp.float32)
    mixed = mixed + weight_new.astype(jnp.float32)[..., None] * new_values[:, :, None, :]
    return mixed.reshape(batch_rows, -1).astype(jnp.bfloat16)


def pick_sum(indicator_matrix, every):
    return jnp.sum(indicator_matrix[:, :, None] * every, axis=1)


def rank_total(partial_rows):
    return lax.psum(partial_rows, "tp").astype(jnp.bfloat16)


def adapter_row_ids(shrunk_part, base_rows, up_factor, indicator_matrix):
    every = jnp.einsum("rk,akc->rac", shrunk_part, up_factor, preferred_element_type=jnp.float32)
    return (base_rows.astype(jnp.float32) + pick_sum(indicator_matrix, every)).astype(jnp.bfloat16)


def adapt_all(
    hidden,
    base_query_proj,
    base_key_proj,
    base_value_proj,
    adapter_down_factors,
    adapter_up_query,
    adapter_up_key_value,
    indicator_matrix,
    rank_extent,
):
    every = jnp.einsum(
        "wb,xbm->wxm", hidden, adapter_down_factors, preferred_element_type=jnp.float32
    )
    shrunk = rank_total(pick_sum(indicator_matrix, every))
    query = adapter_row_ids(
        shrunk[:, :rank_extent], base_query_proj, adapter_up_query, indicator_matrix
    )
    key_new = adapter_row_ids(
        shrunk[:, rank_extent : 2 * rank_extent],
        base_key_proj,
        adapter_up_key_value[:, 0],
        indicator_matrix,
    )
    value_new = adapter_row_ids(
        shrunk[:, 2 * rank_extent :], base_value_proj, adapter_up_key_value[:, 1], indicator_matrix
    )
    return (query, key_new, value_new)


def pick(array, at):
    return lax.dynamic_index_in_dim(array, at, 0, keepdims=False)


def local(
    hidden,
    base_query_proj,
    base_key_proj,
    base_value_proj,
    key_cache,
    value_cache,
    lengths,
    adapter_down_factors,
    adapter_up_query,
    adapter_up_key_value,
    resident,
    request_adapter_id,
    migration_offset,
):
    count = hidden.shape[0]
    moving = migration_offset.shape[0]
    stay = count - moving
    rank_extent = adapter_up_query.shape[1]
    positions = key_cache.shape[1]
    kv_width = base_key_proj.shape[1]
    replicas = lax.axis_size("rep")
    me = lax.axis_index("rep")
    res_row = pick(resident, me)

    offset = [migration_offset[m] for m in range(moving)]
    place = [
        sum((offset[k] < offset[m]).astype(jnp.int32) for k in range(moving) if k != m)
        for m in range(moving)
    ]
    slot_at = [sum(jnp.where(place[m] == p, m, 0) for m in range(moving)) for p in range(moving)]
    offset_at = [
        sum(jnp.where(place[m] == p, offset[m], 0) for m in range(moving)) for p in range(moving)
    ]

    def compute():
        indicator_matrix = (request_adapter_id[:, None] == res_row[None, :]).astype(jnp.float32)
        own_lengths = lax.dynamic_slice_in_dim(lengths, me * count, count)
        query, key_new, value_new = adapt_all(
            hidden,
            base_query_proj,
            base_key_proj,
            base_value_proj,
            adapter_down_factors,
            adapter_up_query,
            adapter_up_key_value,
            indicator_matrix,
            rank_extent,
        )
        completed = attend(query, key_cache, value_cache, key_new, value_new, own_lengths)
        return completed, jnp.concatenate([completed, key_new, value_new], axis=1)

    def big_payload(p):
        row = stay + slot_at[p]
        mine = pick(request_adapter_id, row)
        loaded = sum(
            jnp.where(res_row[n] == mine, n, 0) for n in range(res_row.shape[0])
        )
        return (
            pick(key_cache, row),
            pick(value_cache, row),
            pick(adapter_down_factors, loaded),
            pick(adapter_up_query, loaded),
            pick(adapter_up_key_value, loaded),
        )

    def assemble(completed, small, big):
        rows = []
        for m in range(moving):
            row = small[0]
            for p in range(1, moving):
                row = jnp.where(place[m] == p, small[p], row)
            rows.append(row)
        rows = jnp.stack(rows)
        width = completed.shape[1]
        attended = jnp.concatenate([completed[:stay], rows[:, :width]], axis=0)

        def arrange(part):
            out = []
            for m in range(moving):
                chosen = big[0][part]
                for p in range(1, moving):
                    chosen = jnp.where(place[m] == p, big[p][part], chosen)
                out.append(chosen)
            return jnp.stack(out)

        source = [lax.rem(me - offset[m] + replicas, replicas) for m in range(moving)]
        spots = jnp.stack([pick(lengths, source[m] * count + stay + m) for m in range(moving)])
        at = (jnp.arange(positions, dtype=jnp.int32)[None, :] == spots[:, None])[:, :, None]
        new_keys = rows[:, width : width + kv_width]
        new_values = rows[:, width + kv_width :]
        return (
            attended,
            jnp.where(at, new_keys[:, None, :], arrange(0)),
            jnp.where(at, new_values[:, None, :], arrange(1)),
            arrange(2),
            arrange(3),
            arrange(4),
        )

    table = list(itertools.combinations(range(1, replicas), moving))
    if len(table) <= MOST_JOINT_BRANCHES:

        def branch(by):
            def run():
                big = [
                    tuple(shifted(part, "rep", by[p]) for part in big_payload(p))
                    for p in range(moving)
                ]
                completed, rows = compute()
                small = [shifted(pick(rows, stay + slot_at[p]), "rep", by[p]) for p in range(moving)]
                return assemble(completed, small, big)

            return run

        chosen = sum(
            jnp.where(
                jnp.stack([offset_at[p] == by[p] for p in range(moving)]).all(), i, 0
            )
            for i, by in enumerate(table)
        )
        return lax.switch(chosen, [branch(by) for by in table])

    completed, rows = compute()
    arrived = []
    for p in range(moving):
        payload = (pick(rows, stay + slot_at[p]),) + big_payload(p)
        for level in range((replicas - 1).bit_length()):
            payload = lax.cond(
                jnp.right_shift(offset_at[p], level) % 2 == 1,
                lambda parts, by=1 << level: tuple(shifted(part, "rep", by) for part in parts),
                lambda parts: parts,
                payload,
            )
        arrived.append(payload)
    return assemble(completed, [a[0] for a in arrived], [a[1:] for a in arrived])


def solution(mesh):
    placed = (
        P(("pool", "rep"), "tp"),
        P(("pool", "rep"), "tp"),
        P(("pool", "rep"), "tp"),
        P(("pool", "rep"), "tp"),
        P(("pool", "rep"), None, "tp"),
        P(("pool", "rep"), None, "tp"),
        P("pool"),
        P(("pool", "rep"), "tp", None),
        P(("pool", "rep"), None, "tp"),
        P(("pool", "rep"), None, None, "tp"),
        P("pool", None),
        P(("pool", "rep")),
        P("pool"),
    )
    return jax.shard_map(
        local,
        mesh=mesh,
        in_specs=placed,
        out_specs=(
            P(("pool", "rep"), "tp"),
            P(("pool", "rep"), None, "tp"),
            P(("pool", "rep"), None, "tp"),
            P(("pool", "rep"), "tp", None),
            P(("pool", "rep"), None, "tp"),
            P(("pool", "rep"), None, None, "tp"),
        ),
        check_vma=False,
    )
```

```python
import functools
import itertools
import math

import jax
import jax.numpy as jnp
from jax import lax
from jax.experimental import pallas as pl
from jax.experimental.pallas import tpu as pltpu
from jax.sharding import PartitionSpec as P

HEAD_SIZE = 128
MOST_JOINT_BRANCHES = 6


def shifted(shard, axis, by):
    size = lax.axis_size(axis)
    return lax.ppermute(shard, axis, [(i, (i + by) % size) for i in range(size)])


def attend(query, keys, value_rows, key_new, value_new, lengths_now):
    batch_rows = query.shape[0]
    positions = keys.shape[1]
    kv_heads = key_new.shape[1] // HEAD_SIZE
    group_size = query.shape[1] // (kv_heads * HEAD_SIZE)
    factor = 1.0 / math.sqrt(HEAD_SIZE)
    q_heads = query.reshape(batch_rows, kv_heads, group_size, HEAD_SIZE)
    k_heads = keys.reshape(batch_rows, positions, kv_heads, HEAD_SIZE)
    v_heads = value_rows.reshape(batch_rows, positions, kv_heads, HEAD_SIZE)
    new_keys = key_new.reshape(batch_rows, kv_heads, HEAD_SIZE)
    new_values = value_new.reshape(batch_rows, kv_heads, HEAD_SIZE).astype(jnp.float32)
    scores = (
        jnp.einsum("nhgd,nthd->nhgt", q_heads, k_heads, preferred_element_type=jnp.float32) * factor
    )
    fresh = (
        jnp.einsum("nhgd,nhd->nhg", q_heads, new_keys, preferred_element_type=jnp.float32) * factor
    )
    valid = (jnp.arange(positions, dtype=jnp.int32)[None, :] < lengths_now[:, None])[
        :, None, None, :
    ]
    peak = jnp.maximum(jnp.max(jnp.where(valid, scores, -1e30), axis=-1), fresh)
    raised = jnp.where(valid, jnp.exp(scores - peak[..., None]), 0.0)
    raised_new = jnp.exp(fresh - peak)
    total = jnp.sum(raised, axis=-1) + raised_new
    weights = (raised / total[..., None]).astype(jnp.bfloat16)
    weight_new = (raised_new / total).astype(jnp.bfloat16)
    mixed = jnp.einsum("nhgt,nthd->nhgd", weights, v_heads, preferred_element_type=jnp.float32)
    mixed = mixed + weight_new.astype(jnp.float32)[..., None] * new_values[:, :, None, :]
    return mixed.reshape(batch_rows, -1).astype(jnp.bfloat16)


def pick_sum(indicator_matrix, every):
    return jnp.sum(indicator_matrix[:, :, None] * every, axis=1)


def rank_total(partial_rows):
    return lax.psum(partial_rows, "tp").astype(jnp.bfloat16)


def adapter_row_ids(shrunk_part, base_rows, up_factor, indicator_matrix):
    every = jnp.einsum("rk,akc->rac", shrunk_part, up_factor, preferred_element_type=jnp.float32)
    return (base_rows.astype(jnp.float32) + pick_sum(indicator_matrix, every)).astype(jnp.bfloat16)


def adapt_all(
    hidden,
    base_query_proj,
    base_key_proj,
    base_value_proj,
    adapter_down_factors,
    adapter_up_query,
    adapter_up_key_value,
    indicator_matrix,
    rank_extent,
):
    every = jnp.einsum(
        "wb,xbm->wxm", hidden, adapter_down_factors, preferred_element_type=jnp.float32
    )
    shrunk = rank_total(pick_sum(indicator_matrix, every))
    query = adapter_row_ids(
        shrunk[:, :rank_extent], base_query_proj, adapter_up_query, indicator_matrix
    )
    key_new = adapter_row_ids(
        shrunk[:, rank_extent : 2 * rank_extent],
        base_key_proj,
        adapter_up_key_value[:, 0],
        indicator_matrix,
    )
    value_new = adapter_row_ids(
        shrunk[:, 2 * rank_extent :], base_value_proj, adapter_up_key_value[:, 1], indicator_matrix
    )
    return (query, key_new, value_new)


def pick(array, at):
    return lax.dynamic_index_in_dim(array, at, 0, keepdims=False)


def run_copies(pairs, sems):
    copies = [pltpu.make_async_copy(src, dst, sems.at[i]) for i, (src, dst) in enumerate(pairs)]
    for copy in copies:
        copy.start()
    for copy in copies:
        copy.wait()


def found(values, table):
    at = jnp.int32(0)
    for i, entry in enumerate(table):
        hit = values[0] == entry[0]
        for value, wanted in zip(values[1:], entry[1:]):
            hit = jnp.logical_and(hit, value == wanted)
        at = at + jnp.where(hit, i, 0)
    return at


def gather_kernel(
    table, stay, offset_ref, resident_ref, ids_ref, down_ref, upq_ref, meta_ref, *rest
):
    packs, sems = rest[:-1], rest[-1]
    moving = len(packs)
    me = lax.axis_index("rep")
    offset = [offset_ref[m] for m in range(moving)]
    place = [
        sum((offset[k] < offset[m]).astype(jnp.int32) for k in range(moving) if k != m)
        for m in range(moving)
    ]
    slot_at = [sum(jnp.where(place[m] == p, m, 0) for m in range(moving)) for p in range(moving)]
    pairs = []
    split = down_ref.shape[1]
    for p in range(moving):
        mine = ids_ref[stay + slot_at[p]]
        loaded = sum(
            jnp.where(resident_ref[n, me] == mine, n, 0) for n in range(resident_ref.shape[0])
        )
        meta_ref[2 + p] = slot_at[p]
        pairs.append((down_ref.at[loaded], packs[p].at[pl.ds(0, split)]))
        pairs.append((upq_ref.at[loaded], packs[p].at[pl.ds(split, upq_ref.shape[1])]))
    copies = [pltpu.make_async_copy(src, dst, sems.at[i]) for i, (src, dst) in enumerate(pairs)]
    for copy in copies:
        copy.start()
    offset_at = [
        sum(jnp.where(place[m] == p, offset[m], 0) for m in range(moving)) for p in range(moving)
    ]
    meta_ref[0] = found(offset_at, table)
    meta_ref[1] = found(slot_at, list(itertools.permutations(range(moving))))
    for copy in copies:
        copy.wait()


def place_kernel(moving, splits, meta_ref, *rest):
    packs, outs, sems = rest[:moving], rest[moving:-1], rest[-1]
    pairs = []
    for p in range(moving):
        slot = meta_ref[2 + p]
        start = 0
        for out, rows in zip(outs, splits):
            pairs.append((packs[p].at[pl.ds(start, rows)], out.at[slot]))
            start += rows
    run_copies(pairs, sems)


def place_packs(meta, packs, splits, memory):
    moving = len(packs)
    width = packs[0].shape[1]
    return pl.pallas_call(
        functools.partial(place_kernel, moving, splits),
        out_shape=[
            jax.ShapeDtypeStruct((moving, rows, width), packs[0].dtype) for rows in splits
        ],
        in_specs=[pl.BlockSpec(memory_space=pltpu.SMEM)]
        + [pl.BlockSpec(memory_space=memory)] * moving,
        out_specs=[pl.BlockSpec(memory_space=pltpu.HBM)] * len(splits),
        scratch_shapes=[pltpu.SemaphoreType.DMA((moving * len(splits),))],
        cost_estimate=pl.CostEstimate(
            flops=0, bytes_accessed=4 * moving * sum(splits) * width, transcendentals=0
        ),
    )(meta, *packs)


def local(
    hidden,
    base_query_proj,
    base_key_proj,
    base_value_proj,
    key_cache,
    value_cache,
    lengths,
    adapter_down_factors,
    adapter_up_query,
    adapter_up_key_value,
    resident,
    request_adapter_id,
    migration_offset,
):
    count, model_part = hidden.shape
    moving = migration_offset.shape[0]
    stay = count - moving
    rank_extent, query_part = adapter_up_query.shape[1:]
    rank_rows = adapter_down_factors.shape[2]
    positions, kv_width = key_cache.shape[1:]
    replicas = lax.axis_size("rep")
    me = lax.axis_index("rep")
    table = list(itertools.combinations(range(1, replicas), moving))
    joint = len(table) <= MOST_JOINT_BRANCHES

    pack_rows = rank_rows + rank_extent
    row_rows = -(-model_part // (16 * kv_width)) * 16
    meta, *factor_packs = pl.pallas_call(
        functools.partial(gather_kernel, table if joint else [], stay),
        out_shape=[jax.ShapeDtypeStruct((2 + moving,), jnp.int32)]
        + [jax.ShapeDtypeStruct((pack_rows, query_part), hidden.dtype)] * moving,
        in_specs=[pl.BlockSpec(memory_space=pltpu.SMEM)] * 3
        + [pl.BlockSpec(memory_space=pl.ANY)] * 2,
        out_specs=[pl.BlockSpec(memory_space=pltpu.SMEM)]
        + [pl.BlockSpec(memory_space=pl.ANY)] * moving,
        scratch_shapes=[pltpu.SemaphoreType.DMA((2 * moving,))],
        cost_estimate=pl.CostEstimate(
            flops=0, bytes_accessed=4 * moving * pack_rows * query_part, transcendentals=0
        ),
    )(
        migration_offset,
        resident.T,
        request_adapter_id,
        jnp.swapaxes(adapter_down_factors, 1, 2),
        adapter_up_query,
    )

    def compute(slots):
        res_row = pick(resident, me)
        indicator_matrix = (request_adapter_id[:, None] == res_row[None, :]).astype(jnp.float32)
        own_lengths = lax.dynamic_slice_in_dim(lengths, me * count, count)
        query, key_new, value_new = adapt_all(
            hidden,
            base_query_proj,
            base_key_proj,
            base_value_proj,
            adapter_down_factors,
            adapter_up_query,
            adapter_up_key_value,
            indicator_matrix,
            rank_extent,
        )
        completed = attend(query, key_cache, value_cache, key_new, value_new, own_lengths)
        packs = []
        for slot in slots:
            row = stay + slot
            at = (jnp.arange(positions, dtype=jnp.int32) == own_lengths[row])[:, None]
            up_pair = sum(
                jnp.where(indicator_matrix[row, n] == 1, adapter_up_key_value[n], 0)
                for n in range(res_row.shape[0])
            )
            packs.append(
                jnp.concatenate(
                    [
                        jnp.where(at, key_new[row][None, :], key_cache[row]),
                        jnp.where(at, value_new[row][None, :], value_cache[row]),
                        up_pair.reshape(-1, kv_width),
                        jnp.pad(
                            completed[row].reshape(-1, kv_width),
                            ((0, row_rows - model_part // kv_width), (0, 0)),
                        ),
                    ]
                )
            )
        return (completed, *packs)

    def compute_now():
        orders = itertools.permutations(range(moving))
        return lax.switch(meta[1], [functools.partial(compute, slots) for slots in orders])

    def assemble(completed, cache_packs, factor_packs):
        down, upq = place_packs(meta, factor_packs, (rank_rows, rank_extent), pltpu.HBM)
        keys, value_rows, up_pair, came = place_packs(
            meta, cache_packs, (positions, positions, 2 * rank_extent, row_rows), pltpu.VMEM
        )
        rows = came.reshape(moving, -1)[:, :model_part]
        return (
            jnp.concatenate([completed[:stay], rows], axis=0),
            keys,
            value_rows,
            jnp.swapaxes(down, 1, 2),
            upq,
            up_pair.reshape(moving, 2, rank_extent, kv_width),
        )

    if joint:

        def branch(by):
            def run():
                factors = [shifted(factor_packs[p], "rep", by[p]) for p in range(moving)]
                completed, *packs = compute_now()
                caches = [shifted(packs[p], "rep", by[p]) for p in range(moving)]
                return assemble(completed, caches, factors)

            return run

        return lax.switch(meta[0], [branch(by) for by in table])

    completed, *packs = compute_now()
    caches, factors = [], []
    for p in range(moving):
        payload = (packs[p], factor_packs[p])
        by_now = pick(migration_offset, meta[2 + p])
        for level in range((replicas - 1).bit_length()):
            payload = lax.cond(
                jnp.right_shift(by_now, level) % 2 == 1,
                lambda parts, by=1 << level: tuple(shifted(part, "rep", by) for part in parts),
                lambda parts: parts,
                payload,
            )
        caches.append(payload[0])
        factors.append(payload[1])
    return assemble(completed, caches, factors)


def solution(mesh):
    placed = (
        P(("pool", "rep"), "tp"),
        P(("pool", "rep"), "tp"),
        P(("pool", "rep"), "tp"),
        P(("pool", "rep"), "tp"),
        P(("pool", "rep"), None, "tp"),
        P(("pool", "rep"), None, "tp"),
        P("pool"),
        P(("pool", "rep"), "tp", None),
        P(("pool", "rep"), None, "tp"),
        P(("pool", "rep"), None, None, "tp"),
        P("pool", None),
        P(("pool", "rep")),
        P("pool"),
    )
    return jax.shard_map(
        local,
        mesh=mesh,
        in_specs=placed,
        out_specs=(
            P(("pool", "rep"), "tp"),
            P(("pool", "rep"), None, "tp"),
            P(("pool", "rep"), None, "tp"),
            P(("pool", "rep"), "tp", None),
            P(("pool", "rep"), None, "tp"),
            P(("pool", "rep"), None, None, "tp"),
        ),
        check_vma=False,
    )
```

```python
import functools
import itertools
import math

import jax
import jax.numpy as jnp
from jax import lax
from jax.experimental import pallas as pl
from jax.experimental.pallas import tpu as pltpu
from jax.sharding import PartitionSpec as P

HEAD_SIZE = 128
MOST_JOINT_BRANCHES = 6
KERNEL_VMEM = 8 << 20


def shifted(shard, axis, by):
    size = lax.axis_size(axis)
    return lax.ppermute(shard, axis, [(i, (i + by) % size) for i in range(size)])


def attend(query, keys, value_rows, key_new, value_new, lengths_now):
    batch_rows = query.shape[0]
    positions = keys.shape[1]
    kv_heads = key_new.shape[1] // HEAD_SIZE
    group_size = query.shape[1] // (kv_heads * HEAD_SIZE)
    factor = 1.0 / math.sqrt(HEAD_SIZE)
    q_heads = query.reshape(batch_rows, kv_heads, group_size, HEAD_SIZE)
    k_heads = keys.reshape(batch_rows, positions, kv_heads, HEAD_SIZE)
    v_heads = value_rows.reshape(batch_rows, positions, kv_heads, HEAD_SIZE)
    new_keys = key_new.reshape(batch_rows, kv_heads, HEAD_SIZE)
    new_values = value_new.reshape(batch_rows, kv_heads, HEAD_SIZE).astype(jnp.float32)
    scores = (
        jnp.einsum("nhgd,nthd->nhgt", q_heads, k_heads, preferred_element_type=jnp.float32) * factor
    )
    fresh = (
        jnp.einsum("nhgd,nhd->nhg", q_heads, new_keys, preferred_element_type=jnp.float32) * factor
    )
    valid = (jnp.arange(positions, dtype=jnp.int32)[None, :] < lengths_now[:, None])[
        :, None, None, :
    ]
    peak = jnp.maximum(jnp.max(jnp.where(valid, scores, -1e30), axis=-1), fresh)
    raised = jnp.where(valid, jnp.exp(scores - peak[..., None]), 0.0)
    raised_new = jnp.exp(fresh - peak)
    total = jnp.sum(raised, axis=-1) + raised_new
    weights = (raised / total[..., None]).astype(jnp.bfloat16)
    weight_new = (raised_new / total).astype(jnp.bfloat16)
    mixed = jnp.einsum("nhgt,nthd->nhgd", weights, v_heads, preferred_element_type=jnp.float32)
    mixed = mixed + weight_new.astype(jnp.float32)[..., None] * new_values[:, :, None, :]
    return mixed.reshape(batch_rows, -1).astype(jnp.bfloat16)


def pick_sum(indicator_matrix, every):
    return jnp.sum(indicator_matrix[:, :, None] * every, axis=1)


def rank_total(partial_rows):
    return lax.psum(partial_rows, "tp").astype(jnp.bfloat16)


def adapter_row_ids(shrunk_part, base_rows, up_factor, indicator_matrix):
    every = jnp.einsum("rk,akc->rac", shrunk_part, up_factor, preferred_element_type=jnp.float32)
    return (base_rows.astype(jnp.float32) + pick_sum(indicator_matrix, every)).astype(jnp.bfloat16)


def adapt_all(
    hidden,
    base_query_proj,
    base_key_proj,
    base_value_proj,
    adapter_down_factors,
    adapter_up_query,
    adapter_up_key_value,
    indicator_matrix,
    rank_extent,
):
    every = jnp.einsum(
        "wb,xbm->wxm", hidden, adapter_down_factors, preferred_element_type=jnp.float32
    )
    shrunk = rank_total(pick_sum(indicator_matrix, every))
    query = adapter_row_ids(
        shrunk[:, :rank_extent], base_query_proj, adapter_up_query, indicator_matrix
    )
    key_new = adapter_row_ids(
        shrunk[:, rank_extent : 2 * rank_extent],
        base_key_proj,
        adapter_up_key_value[:, 0],
        indicator_matrix,
    )
    value_new = adapter_row_ids(
        shrunk[:, 2 * rank_extent :], base_value_proj, adapter_up_key_value[:, 1], indicator_matrix
    )
    return (query, key_new, value_new)


def pick(array, at):
    return lax.dynamic_index_in_dim(array, at, 0, keepdims=False)


def run_copies(pairs, sems):
    copies = [pltpu.make_async_copy(src, dst, sems.at[i]) for i, (src, dst) in enumerate(pairs)]
    for copy in copies:
        copy.start()
    for copy in copies:
        copy.wait()


def found(values, table):
    at = jnp.int32(0)
    for i, entry in enumerate(table):
        hit = values[0] == entry[0]
        for value, wanted in zip(values[1:], entry[1:]):
            hit = jnp.logical_and(hit, value == wanted)
        at = at + jnp.where(hit, i, 0)
    return at


def gather_kernel(
    table, stay, offset_ref, resident_ref, ids_ref, down_ref, upq_ref, meta_ref, *rest
):
    packs, sems = rest[:-1], rest[-1]
    moving = len(packs)
    me = lax.axis_index("rep")
    offset = [offset_ref[m] for m in range(moving)]
    place = [
        sum((offset[k] < offset[m]).astype(jnp.int32) for k in range(moving) if k != m)
        for m in range(moving)
    ]
    slot_at = [sum(jnp.where(place[m] == p, m, 0) for m in range(moving)) for p in range(moving)]
    pairs = []
    split = down_ref.shape[1]
    for p in range(moving):
        mine = ids_ref[stay + slot_at[p]]
        loaded = sum(
            jnp.where(resident_ref[n, me] == mine, n, 0) for n in range(resident_ref.shape[0])
        )
        meta_ref[2 + p] = slot_at[p]
        pairs.append((down_ref.at[loaded], packs[p].at[pl.ds(0, split)]))
        pairs.append((upq_ref.at[loaded], packs[p].at[pl.ds(split, upq_ref.shape[1])]))
    copies = [pltpu.make_async_copy(src, dst, sems.at[i]) for i, (src, dst) in enumerate(pairs)]
    for copy in copies:
        copy.start()
    offset_at = [
        sum(jnp.where(place[m] == p, offset[m], 0) for m in range(moving)) for p in range(moving)
    ]
    meta_ref[0] = found(offset_at, table)
    meta_ref[1] = found(slot_at, list(itertools.permutations(range(moving))))
    for copy in copies:
        copy.wait()


def place_kernel(moving, splits, meta_ref, *rest):
    packs, outs, sems = rest[:moving], rest[moving:-1], rest[-1]
    pairs = []
    for p in range(moving):
        slot = meta_ref[2 + p]
        start = 0
        for out, rows in zip(outs, splits):
            pairs.append((packs[p].at[pl.ds(start, rows)], out.at[slot]))
            start += rows
    run_copies(pairs, sems)


def place_packs(meta, packs, splits):
    moving = len(packs)
    width = packs[0].shape[1]
    return pl.pallas_call(
        functools.partial(place_kernel, moving, splits),
        out_shape=[
            jax.ShapeDtypeStruct((moving, rows, width), packs[0].dtype) for rows in splits
        ],
        in_specs=[pl.BlockSpec(memory_space=pltpu.SMEM)]
        + [pl.BlockSpec(memory_space=pltpu.VMEM)] * moving,
        out_specs=[pl.BlockSpec(memory_space=pltpu.HBM)] * len(splits),
        scratch_shapes=[pltpu.SemaphoreType.DMA((moving * len(splits),))],
        compiler_params=pltpu.CompilerParams(vmem_limit_bytes=KERNEL_VMEM),
        cost_estimate=pl.CostEstimate(
            flops=0, bytes_accessed=4 * moving * sum(splits) * width, transcendentals=0
        ),
    )(meta, *packs)


def local(
    hidden,
    base_query_proj,
    base_key_proj,
    base_value_proj,
    key_cache,
    value_cache,
    lengths,
    adapter_down_factors,
    adapter_up_query,
    adapter_up_key_value,
    resident,
    request_adapter_id,
    migration_offset,
):
    count, model_part = hidden.shape
    moving = migration_offset.shape[0]
    stay = count - moving
    rank_extent, query_part = adapter_up_query.shape[1:]
    rank_rows = adapter_down_factors.shape[2]
    positions, kv_width = key_cache.shape[1:]
    replicas = lax.axis_size("rep")
    me = lax.axis_index("rep")
    table = list(itertools.combinations(range(1, replicas), moving))
    joint = len(table) <= MOST_JOINT_BRANCHES

    pack_rows = rank_rows + rank_extent
    row_rows = -(-model_part // (16 * kv_width)) * 16
    meta, *factor_packs = pl.pallas_call(
        functools.partial(gather_kernel, table if joint else [], stay),
        out_shape=[jax.ShapeDtypeStruct((2 + moving,), jnp.int32)]
        + [jax.ShapeDtypeStruct((pack_rows, query_part), hidden.dtype)] * moving,
        in_specs=[pl.BlockSpec(memory_space=pltpu.SMEM)] * 3
        + [pl.BlockSpec(memory_space=pl.ANY)] * 2,
        out_specs=[pl.BlockSpec(memory_space=pltpu.SMEM)]
        + [pl.BlockSpec(memory_space=pltpu.VMEM)] * moving,
        scratch_shapes=[pltpu.SemaphoreType.DMA((2 * moving,))],
        compiler_params=pltpu.CompilerParams(vmem_limit_bytes=KERNEL_VMEM),
        cost_estimate=pl.CostEstimate(
            flops=0, bytes_accessed=4 * moving * pack_rows * query_part, transcendentals=0
        ),
    )(
        migration_offset,
        resident.T,
        request_adapter_id,
        jnp.swapaxes(adapter_down_factors, 1, 2),
        adapter_up_query,
    )

    def compute(slots):
        res_row = pick(resident, me)
        indicator_matrix = (request_adapter_id[:, None] == res_row[None, :]).astype(jnp.float32)
        own_lengths = lax.dynamic_slice_in_dim(lengths, me * count, count)
        query, key_new, value_new = adapt_all(
            hidden,
            base_query_proj,
            base_key_proj,
            base_value_proj,
            adapter_down_factors,
            adapter_up_query,
            adapter_up_key_value,
            indicator_matrix,
            rank_extent,
        )
        completed = attend(query, key_cache, value_cache, key_new, value_new, own_lengths)
        packs = []
        for slot in slots:
            row = stay + slot
            at = (jnp.arange(positions, dtype=jnp.int32) == own_lengths[row])[:, None]
            up_pair = sum(
                jnp.where(indicator_matrix[row, n] == 1, adapter_up_key_value[n], 0)
                for n in range(res_row.shape[0])
            )
            packs.append(
                jnp.concatenate(
                    [
                        jnp.where(at, key_new[row][None, :], key_cache[row]),
                        jnp.where(at, value_new[row][None, :], value_cache[row]),
                        up_pair.reshape(-1, kv_width),
                        jnp.pad(
                            completed[row].reshape(-1, kv_width),
                            ((0, row_rows - model_part // kv_width), (0, 0)),
                        ),
                    ]
                )
            )
        return (completed, *packs)

    def compute_now():
        orders = itertools.permutations(range(moving))
        return lax.switch(meta[1], [functools.partial(compute, slots) for slots in orders])

    def assemble(completed, cache_packs, factor_packs):
        down, upq = place_packs(meta, factor_packs, (rank_rows, rank_extent))
        keys, value_rows, up_pair, came = place_packs(
            meta, cache_packs, (positions, positions, 2 * rank_extent, row_rows)
        )
        rows = came.reshape(moving, -1)[:, :model_part]
        return (
            jnp.concatenate([completed[:stay], rows], axis=0),
            keys,
            value_rows,
            jnp.swapaxes(down, 1, 2),
            upq,
            up_pair.reshape(moving, 2, rank_extent, kv_width),
        )

    if joint:

        def branch(by):
            def run():
                factors = [shifted(factor_packs[p], "rep", by[p]) for p in range(moving)]
                completed, *packs = compute_now()
                caches = [shifted(packs[p], "rep", by[p]) for p in range(moving)]
                return assemble(completed, caches, factors)

            return run

        return lax.switch(meta[0], [branch(by) for by in table])

    completed, *packs = compute_now()
    caches, factors = [], []
    for p in range(moving):
        payload = (packs[p], factor_packs[p])
        by_now = pick(migration_offset, meta[2 + p])
        for level in range((replicas - 1).bit_length()):
            payload = lax.cond(
                jnp.right_shift(by_now, level) % 2 == 1,
                lambda parts, by=1 << level: tuple(shifted(part, "rep", by) for part in parts),
                lambda parts: parts,
                payload,
            )
        caches.append(payload[0])
        factors.append(payload[1])
    return assemble(completed, caches, factors)


def solution(mesh):
    placed = (
        P(("pool", "rep"), "tp"),
        P(("pool", "rep"), "tp"),
        P(("pool", "rep"), "tp"),
        P(("pool", "rep"), "tp"),
        P(("pool", "rep"), None, "tp"),
        P(("pool", "rep"), None, "tp"),
        P("pool"),
        P(("pool", "rep"), "tp", None),
        P(("pool", "rep"), None, "tp"),
        P(("pool", "rep"), None, None, "tp"),
        P("pool", None),
        P(("pool", "rep")),
        P("pool"),
    )
    return jax.shard_map(
        local,
        mesh=mesh,
        in_specs=placed,
        out_specs=(
            P(("pool", "rep"), "tp"),
            P(("pool", "rep"), None, "tp"),
            P(("pool", "rep"), None, "tp"),
            P(("pool", "rep"), "tp", None),
            P(("pool", "rep"), None, "tp"),
            P(("pool", "rep"), None, None, "tp"),
        ),
        check_vma=False,
    )
```

```python
import functools
import itertools
import math

import jax
import jax.numpy as jnp
from jax import lax
from jax.experimental import pallas as pl
from jax.experimental.pallas import tpu as pltpu
from jax.sharding import PartitionSpec as P

HEAD_SIZE = 128
MOST_PAIRS = 6
KERNEL_VMEM = 8 << 20


def shifted(shard, axis, by):
    size = lax.axis_size(axis)
    return lax.ppermute(shard, axis, [(i, (i + by) % size) for i in range(size)])


def attend(query, keys, value_rows, key_new, value_new, lengths_now):
    batch_rows = query.shape[0]
    positions = keys.shape[1]
    kv_heads = key_new.shape[1] // HEAD_SIZE
    group_size = query.shape[1] // (kv_heads * HEAD_SIZE)
    factor = 1.0 / math.sqrt(HEAD_SIZE)
    q_heads = query.reshape(batch_rows, kv_heads, group_size, HEAD_SIZE)
    k_heads = keys.reshape(batch_rows, positions, kv_heads, HEAD_SIZE)
    v_heads = value_rows.reshape(batch_rows, positions, kv_heads, HEAD_SIZE)
    new_keys = key_new.reshape(batch_rows, kv_heads, HEAD_SIZE)
    new_values = value_new.reshape(batch_rows, kv_heads, HEAD_SIZE).astype(jnp.float32)
    scores = (
        jnp.einsum("nhgd,nthd->nhgt", q_heads, k_heads, preferred_element_type=jnp.float32) * factor
    )
    fresh = (
        jnp.einsum("nhgd,nhd->nhg", q_heads, new_keys, preferred_element_type=jnp.float32) * factor
    )
    valid = (jnp.arange(positions, dtype=jnp.int32)[None, :] < lengths_now[:, None])[
        :, None, None, :
    ]
    peak = jnp.maximum(jnp.max(jnp.where(valid, scores, -1e30), axis=-1), fresh)
    raised = jnp.where(valid, jnp.exp(scores - peak[..., None]), 0.0)
    raised_new = jnp.exp(fresh - peak)
    total = jnp.sum(raised, axis=-1) + raised_new
    weights = (raised / total[..., None]).astype(jnp.bfloat16)
    weight_new = (raised_new / total).astype(jnp.bfloat16)
    mixed = jnp.einsum("nhgt,nthd->nhgd", weights, v_heads, preferred_element_type=jnp.float32)
    mixed = mixed + weight_new.astype(jnp.float32)[..., None] * new_values[:, :, None, :]
    return mixed.reshape(batch_rows, -1).astype(jnp.bfloat16)


def pick_sum(indicator_matrix, every):
    return jnp.sum(indicator_matrix[:, :, None] * every, axis=1)


def rank_total(partial_rows):
    return lax.psum(partial_rows, "tp").astype(jnp.bfloat16)


def adapter_row_ids(shrunk_part, base_rows, up_factor, indicator_matrix):
    every = jnp.einsum("rk,akc->rac", shrunk_part, up_factor, preferred_element_type=jnp.float32)
    return (base_rows.astype(jnp.float32) + pick_sum(indicator_matrix, every)).astype(jnp.bfloat16)


def adapt_all(
    hidden,
    base_query_proj,
    base_key_proj,
    base_value_proj,
    adapter_down_factors,
    adapter_up_query,
    adapter_up_key_value,
    indicator_matrix,
    rank_extent,
):
    every = jnp.einsum(
        "wb,xbm->wxm", hidden, adapter_down_factors, preferred_element_type=jnp.float32
    )
    shrunk = rank_total(pick_sum(indicator_matrix, every))
    query = adapter_row_ids(
        shrunk[:, :rank_extent], base_query_proj, adapter_up_query, indicator_matrix
    )
    key_new = adapter_row_ids(
        shrunk[:, rank_extent : 2 * rank_extent],
        base_key_proj,
        adapter_up_key_value[:, 0],
        indicator_matrix,
    )
    value_new = adapter_row_ids(
        shrunk[:, 2 * rank_extent :], base_value_proj, adapter_up_key_value[:, 1], indicator_matrix
    )
    return (query, key_new, value_new)


def pick(array, at):
    return lax.dynamic_index_in_dim(array, at, 0, keepdims=False)


def run_copies(pairs, sems):
    copies = [pltpu.make_async_copy(src, dst, sems.at[i]) for i, (src, dst) in enumerate(pairs)]
    for copy in copies:
        copy.start()
    for copy in copies:
        copy.wait()


def found(values, table):
    at = jnp.int32(0)
    for i, entry in enumerate(table):
        hit = values[0] == entry[0]
        for value, wanted in zip(values[1:], entry[1:]):
            hit = jnp.logical_and(hit, value == wanted)
        at = at + jnp.where(hit, i, 0)
    return at


def gather_kernel(
    table, stay, offset_ref, resident_ref, ids_ref, down_ref, upq_ref, meta_ref, *rest
):
    packs, sems = rest[:-1], rest[-1]
    moving = len(packs)
    me = lax.axis_index("rep")
    offset = [offset_ref[m] for m in range(moving)]
    place = [
        sum((offset[k] < offset[m]).astype(jnp.int32) for k in range(moving) if k != m)
        for m in range(moving)
    ]
    slot_at = [sum(jnp.where(place[m] == p, m, 0) for m in range(moving)) for p in range(moving)]
    pairs = []
    split = down_ref.shape[1]
    for p in range(moving):
        mine = ids_ref[stay + slot_at[p]]
        loaded = sum(
            jnp.where(resident_ref[n, me] == mine, n, 0) for n in range(resident_ref.shape[0])
        )
        meta_ref[2 + p] = slot_at[p]
        pairs.append((down_ref.at[loaded], packs[p].at[pl.ds(0, split)]))
        pairs.append((upq_ref.at[loaded], packs[p].at[pl.ds(split, upq_ref.shape[1])]))
    copies = [pltpu.make_async_copy(src, dst, sems.at[i]) for i, (src, dst) in enumerate(pairs)]
    for copy in copies:
        copy.start()
    offset_at = [
        sum(jnp.where(place[m] == p, offset[m], 0) for m in range(moving)) for p in range(moving)
    ]
    meta_ref[0] = found(offset_at, table)
    meta_ref[1] = found(slot_at, list(itertools.permutations(range(moving))))
    for copy in copies:
        copy.wait()


def place_kernel(splits, piece_rows, meta_ref, *rest):
    pieces = sum(len(rows) for rows in piece_rows)
    packs, outs, sems = list(rest[:pieces]), rest[pieces:-1], rest[-1]
    pairs = []
    for p, rows_of in enumerate(piece_rows):
        slot = meta_ref[2 + p]
        piece_start = 0
        for rows in rows_of:
            pack = packs.pop(0)
            start = 0
            for out, wanted in zip(outs, splits):
                first = max(start, piece_start)
                last = min(start + wanted, piece_start + rows)
                if first < last:
                    pairs.append(
                        (
                            pack.at[pl.ds(first - piece_start, last - first)],
                            out.at[slot, pl.ds(first - start, last - first)],
                        )
                    )
                start += wanted
            piece_start += rows
    run_copies(pairs, sems)


def place_packs(meta, packs, splits):
    moving = len(packs)
    pieces = [piece for pack in packs for piece in pack]
    width = pieces[0].shape[1]
    piece_rows = tuple(tuple(piece.shape[0] for piece in pack) for pack in packs)
    return pl.pallas_call(
        functools.partial(place_kernel, splits, piece_rows),
        out_shape=[
            jax.ShapeDtypeStruct((moving, rows, width), pieces[0].dtype) for rows in splits
        ],
        in_specs=[pl.BlockSpec(memory_space=pltpu.SMEM)]
        + [pl.BlockSpec(memory_space=pltpu.VMEM)] * len(pieces),
        out_specs=[pl.BlockSpec(memory_space=pltpu.HBM)] * len(splits),
        scratch_shapes=[pltpu.SemaphoreType.DMA((len(pieces) * len(splits),))],
        compiler_params=pltpu.CompilerParams(vmem_limit_bytes=KERNEL_VMEM),
        cost_estimate=pl.CostEstimate(
            flops=0, bytes_accessed=4 * moving * sum(splits) * width, transcendentals=0
        ),
    )(meta, *pieces)


def joint_kernel(table, meta_ref, other_ref, joint_ref):
    moving = other_ref.shape[0]
    own = meta_ref[0]
    other = jnp.int32(0)
    for i, entry in enumerate(table):
        hits = sum(
            (other_ref[m] == by).astype(jnp.int32) for m in range(moving) for by in entry
        )
        other = other + jnp.where(hits == moving, i, 0)
    size = len(table)
    first = lax.axis_index("pool") == 0
    joint_ref[0] = jnp.where(first, own * size + other, other * size + own)


def link_load(by, replicas):
    return sum(min(shift, replicas - shift) for shift in by)


def local(
    hidden,
    base_query_proj,
    base_key_proj,
    base_value_proj,
    key_cache,
    value_cache,
    lengths,
    adapter_down_factors,
    adapter_up_query,
    adapter_up_key_value,
    resident,
    request_adapter_id,
    migration_offset,
):
    count, model_part = hidden.shape
    moving = migration_offset.shape[0]
    stay = count - moving
    rank_extent, query_part = adapter_up_query.shape[1:]
    rank_rows = adapter_down_factors.shape[2]
    positions, kv_width = key_cache.shape[1:]
    replicas = lax.axis_size("rep")
    me = lax.axis_index("rep")
    table = list(itertools.combinations(range(1, replicas), moving))
    pools = lax.axis_size("pool")
    joint = pools == 2 and len(table) <= MOST_PAIRS

    pack_rows = rank_rows + rank_extent
    cache_rows = 2 * positions + 2 * rank_extent + -(-model_part // (16 * kv_width)) * 16
    row_rows = -(-model_part // (16 * kv_width)) * 16
    meta, *factor_packs = pl.pallas_call(
        functools.partial(gather_kernel, table if joint else [], stay),
        out_shape=[jax.ShapeDtypeStruct((2 + moving,), jnp.int32)]
        + [jax.ShapeDtypeStruct((pack_rows, query_part), hidden.dtype)] * moving,
        in_specs=[pl.BlockSpec(memory_space=pltpu.SMEM)] * 3
        + [pl.BlockSpec(memory_space=pl.ANY)] * 2,
        out_specs=[pl.BlockSpec(memory_space=pltpu.SMEM)]
        + [pl.BlockSpec(memory_space=pltpu.VMEM)] * moving,
        scratch_shapes=[pltpu.SemaphoreType.DMA((2 * moving,))],
        compiler_params=pltpu.CompilerParams(vmem_limit_bytes=KERNEL_VMEM),
        cost_estimate=pl.CostEstimate(
            flops=0, bytes_accessed=4 * moving * pack_rows * query_part, transcendentals=0
        ),
    )(
        migration_offset,
        resident.T,
        request_adapter_id,
        jnp.swapaxes(adapter_down_factors, 1, 2),
        adapter_up_query,
    )

    def compute(slots):
        res_row = pick(resident, me)
        indicator_matrix = (request_adapter_id[:, None] == res_row[None, :]).astype(jnp.float32)
        own_lengths = lax.dynamic_slice_in_dim(lengths, me * count, count)
        query, key_new, value_new = adapt_all(
            hidden,
            base_query_proj,
            base_key_proj,
            base_value_proj,
            adapter_down_factors,
            adapter_up_query,
            adapter_up_key_value,
            indicator_matrix,
            rank_extent,
        )
        completed = attend(query, key_cache, value_cache, key_new, value_new, own_lengths)
        packs = []
        for slot in slots:
            row = stay + slot
            at = (jnp.arange(positions, dtype=jnp.int32) == own_lengths[row])[:, None]
            up_pair = sum(
                jnp.where(indicator_matrix[row, n] == 1, adapter_up_key_value[n], 0)
                for n in range(res_row.shape[0])
            )
            packs.append(
                jnp.concatenate(
                    [
                        jnp.where(at, key_new[row][None, :], key_cache[row]),
                        jnp.where(at, value_new[row][None, :], value_cache[row]),
                        up_pair.reshape(-1, kv_width),
                        jnp.pad(
                            completed[row].reshape(-1, kv_width),
                            ((0, row_rows - model_part // kv_width), (0, 0)),
                        ),
                    ]
                )
            )
        return (completed, *packs)

    def compute_now():
        orders = itertools.permutations(range(moving))
        return lax.switch(meta[1], [functools.partial(compute, slots) for slots in orders])

    def assemble(completed, cache_packs, factor_packs):
        down, upq = place_packs(meta, factor_packs, (rank_rows, rank_extent))
        slots, down, upq = lax.optimization_barrier((meta, down, upq))
        keys, value_rows, up_pair, came = place_packs(
            slots, [[pack] for pack in cache_packs], (positions, positions, 2 * rank_extent, row_rows)
        )
        rows = came.reshape(moving, -1)[:, :model_part]
        return (
            jnp.concatenate([completed[:stay], rows], axis=0),
            keys,
            value_rows,
            jnp.swapaxes(down, 1, 2),
            upq,
            up_pair.reshape(moving, 2, rank_extent, kv_width),
        )

    if joint:
        other_offset = lax.ppermute(migration_offset, "pool", [(0, 1), (1, 0)])
        chosen = pl.pallas_call(
            functools.partial(joint_kernel, table),
            out_shape=jax.ShapeDtypeStruct((1,), jnp.int32),
            in_specs=[pl.BlockSpec(memory_space=pltpu.SMEM)] * 2,
            out_specs=pl.BlockSpec(memory_space=pltpu.SMEM),
            compiler_params=pltpu.CompilerParams(vmem_limit_bytes=KERNEL_VMEM),
        )(meta, other_offset)

        def sent(array, routes):
            pairs = [
                (start * replicas + r, end * replicas + (r + shift) % replicas)
                for start, end, shift in routes
                for r in range(replicas)
            ]
            return lax.ppermute(array, ("pool", "rep"), pairs)

        def branch(by):
            loads = [link_load(by[q], replicas) for q in range(pools)]
            slow = loads.index(max(loads))
            fast = 1 - slow
            lengths_of = [min(shift, replicas - shift) for shift in by[slow]]
            far = lengths_of.index(max(lengths_of))
            size = pack_rows * query_part + cache_rows * kv_width
            share = (loads[slow] - loads[fast]) / (2 * lengths_of[far])
            relayed = min(int(share * size / query_part) // 16 * 16, pack_rows)
            own_way = [[(q, q, by[q][p]) for q in range(pools)] for p in range(moving)]

            def run():
                factors = [[pack] for pack in factor_packs]
                if relayed:
                    kept = pack_rows - relayed
                    part = factor_packs[far][kept:]
                    across = sent(part, [(slow, fast, 0)])
                    factors[far] = [factor_packs[far][:kept]]
                arrived = [[sent(pack[0], own_way[p])] for p, pack in enumerate(factors)]
                if relayed:
                    came = jnp.where(
                        lax.axis_index("pool") == fast,
                        sent(part, [(fast, fast, by[fast][far])]),
                        sent(across, [(fast, slow, by[slow][far])]),
                    )
                    arrived[far].append(came)
                completed, *packs = compute_now()
                caches = [sent(packs[p], own_way[p]) for p in range(moving)]
                return assemble(completed, caches, arrived)

            return run

        return lax.switch(
            chosen[0], [branch(by) for by in itertools.product(table, repeat=pools)]
        )

    completed, *packs = compute_now()
    caches, factors = [], []
    for p in range(moving):
        payload = (packs[p], factor_packs[p])
        by_now = pick(migration_offset, meta[2 + p])
        for level in range((replicas - 1).bit_length()):
            payload = lax.cond(
                jnp.right_shift(by_now, level) % 2 == 1,
                lambda parts, by=1 << level: tuple(shifted(part, "rep", by) for part in parts),
                lambda parts: parts,
                payload,
            )
        caches.append(payload[0])
        factors.append(payload[1])
    return assemble(completed, caches, [[pack] for pack in factors])


def solution(mesh):
    placed = (
        P(("pool", "rep"), "tp"),
        P(("pool", "rep"), "tp"),
        P(("pool", "rep"), "tp"),
        P(("pool", "rep"), "tp"),
        P(("pool", "rep"), None, "tp"),
        P(("pool", "rep"), None, "tp"),
        P("pool"),
        P(("pool", "rep"), "tp", None),
        P(("pool", "rep"), None, "tp"),
        P(("pool", "rep"), None, None, "tp"),
        P("pool", None),
        P(("pool", "rep")),
        P("pool"),
    )
    return jax.shard_map(
        local,
        mesh=mesh,
        in_specs=placed,
        out_specs=(
            P(("pool", "rep"), "tp"),
            P(("pool", "rep"), None, "tp"),
            P(("pool", "rep"), None, "tp"),
            P(("pool", "rep"), "tp", None),
            P(("pool", "rep"), None, "tp"),
            P(("pool", "rep"), None, None, "tp"),
        ),
        check_vma=False,
    )
```

```python
import functools
import itertools
import math

import jax
import jax.numpy as jnp
from jax import lax
from jax.experimental import pallas as pl
from jax.experimental.pallas import tpu as pltpu
from jax.sharding import PartitionSpec as P

HEAD_SIZE = 128
MOST_PAIRS = 6
KERNEL_VMEM = 8 << 20


def shifted(shard, axis, by):
    size = lax.axis_size(axis)
    return lax.ppermute(shard, axis, [(i, (i + by) % size) for i in range(size)])


def attend(query, keys, value_rows, key_new, value_new, lengths_now):
    batch_rows = query.shape[0]
    positions = keys.shape[1]
    kv_heads = key_new.shape[1] // HEAD_SIZE
    group_size = query.shape[1] // (kv_heads * HEAD_SIZE)
    factor = 1.0 / math.sqrt(HEAD_SIZE)
    q_heads = query.reshape(batch_rows, kv_heads, group_size, HEAD_SIZE)
    k_heads = keys.reshape(batch_rows, positions, kv_heads, HEAD_SIZE)
    v_heads = value_rows.reshape(batch_rows, positions, kv_heads, HEAD_SIZE)
    new_keys = key_new.reshape(batch_rows, kv_heads, HEAD_SIZE)
    new_values = value_new.reshape(batch_rows, kv_heads, HEAD_SIZE).astype(jnp.float32)
    scores = (
        jnp.einsum("nhgd,nthd->nhgt", q_heads, k_heads, preferred_element_type=jnp.float32) * factor
    )
    fresh = (
        jnp.einsum("nhgd,nhd->nhg", q_heads, new_keys, preferred_element_type=jnp.float32) * factor
    )
    valid = (jnp.arange(positions, dtype=jnp.int32)[None, :] < lengths_now[:, None])[
        :, None, None, :
    ]
    peak = jnp.maximum(jnp.max(jnp.where(valid, scores, -1e30), axis=-1), fresh)
    raised = jnp.where(valid, jnp.exp(scores - peak[..., None]), 0.0)
    raised_new = jnp.exp(fresh - peak)
    total = jnp.sum(raised, axis=-1) + raised_new
    weights = (raised / total[..., None]).astype(jnp.bfloat16)
    weight_new = (raised_new / total).astype(jnp.bfloat16)
    mixed = jnp.einsum("nhgt,nthd->nhgd", weights, v_heads, preferred_element_type=jnp.float32)
    mixed = mixed + weight_new.astype(jnp.float32)[..., None] * new_values[:, :, None, :]
    return mixed.reshape(batch_rows, -1).astype(jnp.bfloat16)


def pick_sum(indicator_matrix, every):
    return jnp.sum(indicator_matrix[:, :, None] * every, axis=1)


def rank_total(partial_rows):
    return lax.psum(partial_rows, "tp").astype(jnp.bfloat16)


def adapter_row_ids(shrunk_part, base_rows, up_factor, indicator_matrix):
    every = jnp.einsum("rk,akc->rac", shrunk_part, up_factor, preferred_element_type=jnp.float32)
    return (base_rows.astype(jnp.float32) + pick_sum(indicator_matrix, every)).astype(jnp.bfloat16)


def adapt_all(
    hidden,
    base_query_proj,
    base_key_proj,
    base_value_proj,
    adapter_down_factors,
    adapter_up_query,
    adapter_up_key_value,
    indicator_matrix,
    rank_extent,
):
    every = jnp.einsum(
        "wb,xbm->wxm", hidden, adapter_down_factors, preferred_element_type=jnp.float32
    )
    shrunk = rank_total(pick_sum(indicator_matrix, every))
    query = adapter_row_ids(
        shrunk[:, :rank_extent], base_query_proj, adapter_up_query, indicator_matrix
    )
    key_new = adapter_row_ids(
        shrunk[:, rank_extent : 2 * rank_extent],
        base_key_proj,
        adapter_up_key_value[:, 0],
        indicator_matrix,
    )
    value_new = adapter_row_ids(
        shrunk[:, 2 * rank_extent :], base_value_proj, adapter_up_key_value[:, 1], indicator_matrix
    )
    return (query, key_new, value_new)


def pick(array, at):
    return lax.dynamic_index_in_dim(array, at, 0, keepdims=False)


def found(values, table):
    at = jnp.int32(0)
    for i, entry in enumerate(table):
        hit = values[0] == entry[0]
        for value, wanted in zip(values[1:], entry[1:]):
            hit = jnp.logical_and(hit, value == wanted)
        at = at + jnp.where(hit, i, 0)
    return at


def gather_kernel(
    table, stay, offset_ref, resident_ref, ids_ref, down_ref, upq_ref, meta_ref, *rest
):
    packs, sems = rest[:-1], rest[-1]
    moving = len(packs)
    me = lax.axis_index("rep")
    offset = [offset_ref[m] for m in range(moving)]
    place = [
        sum((offset[k] < offset[m]).astype(jnp.int32) for k in range(moving) if k != m)
        for m in range(moving)
    ]
    slot_at = [sum(jnp.where(place[m] == p, m, 0) for m in range(moving)) for p in range(moving)]
    pairs = []
    split = down_ref.shape[1]
    for p in range(moving):
        mine = ids_ref[stay + slot_at[p]]
        loaded = sum(
            jnp.where(resident_ref[n, me] == mine, n, 0) for n in range(resident_ref.shape[0])
        )
        meta_ref[2 + p] = slot_at[p]
        pairs.append((down_ref.at[loaded], packs[p].at[pl.ds(0, split)]))
        pairs.append((upq_ref.at[loaded], packs[p].at[pl.ds(split, upq_ref.shape[1])]))
    copies = [pltpu.make_async_copy(src, dst, sems.at[i]) for i, (src, dst) in enumerate(pairs)]
    for copy in copies:
        copy.start()
    offset_at = [
        sum(jnp.where(place[m] == p, offset[m], 0) for m in range(moving)) for p in range(moving)
    ]
    meta_ref[0] = found(offset_at, table)
    meta_ref[1] = found(slot_at, list(itertools.permutations(range(moving))))
    for copy in copies:
        copy.wait()


def place_kernel(splits, pieces, meta_ref, *rest):
    packs, outs, sems = rest[: len(pieces)], rest[len(pieces) : -1], rest[-1]
    pool, copies = lax.axis_index("pool"), []
    for pack, (place, first_row, rows, pools) in zip(packs, pieces):
        slot = meta_ref[2 + place]
        start = 0
        for out, wanted in zip(outs, splits):
            first, last = max(start, first_row), min(start + wanted, first_row + rows)
            if first < last:
                copy = pltpu.make_async_copy(
                    pack.at[pl.ds(first - first_row, last - first)],
                    out.at[slot, pl.ds(first - start, last - first)],
                    sems.at[len(copies)],
                )
                copies.append((copy, pools))
            start += wanted

    def each(act):
        for copy, pools in copies:
            if pools is None:
                act(copy)
            else:
                pl.when(sum((pool == q).astype(jnp.int32) for q in pools) > 0)(
                    functools.partial(act, copy)
                )

    each(lambda copy: copy.start())
    each(lambda copy: copy.wait())


def place_packs(meta, moving, pieces, splits):
    arrays = [piece[0] for piece in pieces]
    width = arrays[0].shape[1]
    where = tuple((place, first, array.shape[0], pools) for array, place, first, pools in pieces)
    return pl.pallas_call(
        functools.partial(place_kernel, splits, where),
        out_shape=[
            jax.ShapeDtypeStruct((moving, rows, width), arrays[0].dtype) for rows in splits
        ],
        in_specs=[pl.BlockSpec(memory_space=pltpu.SMEM)]
        + [pl.BlockSpec(memory_space=pltpu.VMEM)] * len(arrays),
        out_specs=[pl.BlockSpec(memory_space=pltpu.HBM)] * len(splits),
        scratch_shapes=[pltpu.SemaphoreType.DMA((len(arrays) * len(splits),))],
        compiler_params=pltpu.CompilerParams(vmem_limit_bytes=KERNEL_VMEM),
        cost_estimate=pl.CostEstimate(
            flops=0, bytes_accessed=4 * moving * sum(splits) * width, transcendentals=0
        ),
    )(meta, *arrays)


def joint_kernel(table, meta_ref, other_ref, joint_ref):
    moving = other_ref.shape[0]
    own = meta_ref[0]
    other = jnp.int32(0)
    for i, entry in enumerate(table):
        hits = sum(
            (other_ref[m] == by).astype(jnp.int32) for m in range(moving) for by in entry
        )
        other = other + jnp.where(hits == moving, i, 0)
    size = len(table)
    first = lax.axis_index("pool") == 0
    joint_ref[0] = jnp.where(first, own * size + other, other * size + own)


def distance(shift, replicas):
    return min(shift % replicas, -shift % replicas)


def local(
    hidden,
    base_query_proj,
    base_key_proj,
    base_value_proj,
    key_cache,
    value_cache,
    lengths,
    adapter_down_factors,
    adapter_up_query,
    adapter_up_key_value,
    resident,
    request_adapter_id,
    migration_offset,
):
    count, model_part = hidden.shape
    moving = migration_offset.shape[0]
    stay = count - moving
    rank_extent, query_part = adapter_up_query.shape[1:]
    rank_rows = adapter_down_factors.shape[2]
    positions, kv_width = key_cache.shape[1:]
    replicas = lax.axis_size("rep")
    me = lax.axis_index("rep")
    table = list(itertools.combinations(range(1, replicas), moving))
    pools = lax.axis_size("pool")
    joint = pools == 2 and moving == 2 and len(table) <= MOST_PAIRS

    pack_rows = rank_rows + rank_extent
    cache_rows = 2 * positions + 2 * rank_extent + -(-model_part // (16 * kv_width)) * 16
    row_rows = -(-model_part // (16 * kv_width)) * 16
    meta, *factor_packs = pl.pallas_call(
        functools.partial(gather_kernel, table if joint else [], stay),
        out_shape=[jax.ShapeDtypeStruct((2 + moving,), jnp.int32)]
        + [jax.ShapeDtypeStruct((pack_rows, query_part), hidden.dtype)] * moving,
        in_specs=[pl.BlockSpec(memory_space=pltpu.SMEM)] * 3
        + [pl.BlockSpec(memory_space=pl.ANY)] * 2,
        out_specs=[pl.BlockSpec(memory_space=pltpu.SMEM)]
        + [pl.BlockSpec(memory_space=pltpu.VMEM)] * moving,
        scratch_shapes=[pltpu.SemaphoreType.DMA((2 * moving,))],
        compiler_params=pltpu.CompilerParams(vmem_limit_bytes=KERNEL_VMEM),
        cost_estimate=pl.CostEstimate(
            flops=0, bytes_accessed=4 * moving * pack_rows * query_part, transcendentals=0
        ),
    )(
        migration_offset,
        resident.T,
        request_adapter_id,
        jnp.swapaxes(adapter_down_factors, 1, 2),
        adapter_up_query,
    )

    def compute(slots):
        res_row = pick(resident, me)
        indicator_matrix = (request_adapter_id[:, None] == res_row[None, :]).astype(jnp.float32)
        own_lengths = lax.dynamic_slice_in_dim(lengths, me * count, count)
        query, key_new, value_new = adapt_all(
            hidden,
            base_query_proj,
            base_key_proj,
            base_value_proj,
            adapter_down_factors,
            adapter_up_query,
            adapter_up_key_value,
            indicator_matrix,
            rank_extent,
        )
        completed = attend(query, key_cache, value_cache, key_new, value_new, own_lengths)
        packs = []
        for slot in slots:
            row = stay + slot
            at = (jnp.arange(positions, dtype=jnp.int32) == own_lengths[row])[:, None]
            up_pair = sum(
                jnp.where(indicator_matrix[row, n] == 1, adapter_up_key_value[n], 0)
                for n in range(res_row.shape[0])
            )
            packs.append(
                jnp.concatenate(
                    [
                        jnp.where(at, key_new[row][None, :], key_cache[row]),
                        jnp.where(at, value_new[row][None, :], value_cache[row]),
                        up_pair.reshape(-1, kv_width),
                        jnp.pad(
                            completed[row].reshape(-1, kv_width),
                            ((0, row_rows - model_part // kv_width), (0, 0)),
                        ),
                    ]
                )
            )
        return (completed, *packs)

    def compute_now():
        orders = itertools.permutations(range(moving))
        return lax.switch(meta[1], [functools.partial(compute, slots) for slots in orders])

    def assemble(completed, cache_pieces, factor_pieces):
        down, upq = place_packs(meta, moving, factor_pieces, (rank_rows, rank_extent))
        slots, down, upq = lax.optimization_barrier((meta, down, upq))
        keys, value_rows, up_pair, came = place_packs(
            slots, moving, cache_pieces, (positions, positions, 2 * rank_extent, row_rows)
        )
        rows = came.reshape(moving, -1)[:, :model_part]
        return (
            jnp.concatenate([completed[:stay], rows], axis=0),
            keys,
            value_rows,
            jnp.swapaxes(down, 1, 2),
            upq,
            up_pair.reshape(moving, 2, rank_extent, kv_width),
        )

    if joint:
        first_hop = (1, -1)
        halfway = [shifted(factor_packs[p], "rep", first_hop[p]) for p in range(moving)]
        other_offset = lax.ppermute(migration_offset, "pool", [(0, 1), (1, 0)])
        chosen = pl.pallas_call(
            functools.partial(joint_kernel, table),
            out_shape=jax.ShapeDtypeStruct((1,), jnp.int32),
            in_specs=[pl.BlockSpec(memory_space=pltpu.SMEM)] * 2,
            out_specs=pl.BlockSpec(memory_space=pltpu.SMEM),
            compiler_params=pltpu.CompilerParams(vmem_limit_bytes=KERNEL_VMEM),
        )(meta, other_offset)
        completed, *cache_packs = compute_now()

        def sent(array, routes):
            pairs = [
                (start * replicas + r, end * replicas + (r + shift) % replicas)
                for start, end, shift in routes
                for r in range(replicas)
            ]
            return lax.ppermute(array, ("pool", "rep"), pairs)

        def branch(by):
            left = [[(by[q][p] - first_hop[p]) % replicas for p in range(moving)] for q in (0, 1)]
            loads = [
                sum(
                    distance(by[q][p], replicas) * cache_rows * kv_width
                    + distance(left[q][p], replicas) * pack_rows * query_part
                    for p in range(moving)
                )
                for q in (0, 1)
            ]
            slow = loads.index(max(loads))
            fast = 1 - slow
            hops = [distance(shift, replicas) for shift in by[slow]]
            far = hops.index(max(hops))
            share = (loads[slow] - loads[fast]) / (2 * hops[far] * kv_width)
            relayed = min(int(share) // 16 * 16, cache_rows - 16)
            kept = cache_rows - relayed

            def run():
                factor_pieces, cache_pieces = [], []
                for p in range(moving):
                    going = [q for q in (0, 1) if left[q][p] != 0]
                    if going:
                        hop = sent(halfway[p], [(q, q, left[q][p]) for q in going])
                        factor_pieces.append((hop, p, 0, going))
                    there = [q for q in (0, 1) if q not in going]
                    if there:
                        factor_pieces.append((halfway[p], p, 0, there))
                    whole = cache_packs[p]
                    own_way = [(q, q, by[q][p]) for q in (0, 1)]
                    if p == far and relayed:
                        part = whole[kept:]
                        across = sent(part, [(slow, fast, 0)])
                        cache_pieces.append((sent(whole[:kept], own_way), p, 0, None))
                        direct = sent(part, [(fast, fast, by[fast][p])])
                        cache_pieces.append((direct, p, kept, [fast]))
                        round_about = sent(across, [(fast, slow, by[slow][p])])
                        cache_pieces.append((round_about, p, kept, [slow]))
                    else:
                        cache_pieces.append((sent(whole, own_way), p, 0, None))
                return assemble(completed, cache_pieces, factor_pieces)

            return run

        return lax.switch(
            chosen[0], [branch(by) for by in itertools.product(table, repeat=pools)]
        )

    completed, *packs = compute_now()
    caches, factors = [], []
    for p in range(moving):
        payload = (packs[p], factor_packs[p])
        by_now = pick(migration_offset, meta[2 + p])
        for level in range((replicas - 1).bit_length()):
            payload = lax.cond(
                jnp.right_shift(by_now, level) % 2 == 1,
                lambda parts, by=1 << level: tuple(shifted(part, "rep", by) for part in parts),
                lambda parts: parts,
                payload,
            )
        caches.append(payload[0])
        factors.append(payload[1])
    return assemble(
        completed,
        [(pack, p, 0, None) for p, pack in enumerate(caches)],
        [(pack, p, 0, None) for p, pack in enumerate(factors)],
    )


def solution(mesh):
    placed = (
        P(("pool", "rep"), "tp"),
        P(("pool", "rep"), "tp"),
        P(("pool", "rep"), "tp"),
        P(("pool", "rep"), "tp"),
        P(("pool", "rep"), None, "tp"),
        P(("pool", "rep"), None, "tp"),
        P("pool"),
        P(("pool", "rep"), "tp", None),
        P(("pool", "rep"), None, "tp"),
        P(("pool", "rep"), None, None, "tp"),
        P("pool", None),
        P(("pool", "rep")),
        P("pool"),
    )
    return jax.shard_map(
        local,
        mesh=mesh,
        in_specs=placed,
        out_specs=(
            P(("pool", "rep"), "tp"),
            P(("pool", "rep"), None, "tp"),
            P(("pool", "rep"), None, "tp"),
            P(("pool", "rep"), "tp", None),
            P(("pool", "rep"), None, "tp"),
            P(("pool", "rep"), None, None, "tp"),
        ),
        check_vma=False,
    )
```

```python
import functools
import itertools
import math

import jax
import jax.numpy as jnp
from jax import lax
from jax.experimental import pallas as pl
from jax.experimental.pallas import tpu as pltpu
from jax.sharding import PartitionSpec as P

HEAD_SIZE = 128
MOST_PAIRS = 6
KERNEL_VMEM = 8 << 20


def shifted(shard, axis, by):
    size = lax.axis_size(axis)
    return lax.ppermute(shard, axis, [(i, (i + by) % size) for i in range(size)])


def attend(query, keys, value_rows, key_new, value_new, lengths_now):
    batch_rows = query.shape[0]
    positions = keys.shape[1]
    kv_heads = key_new.shape[1] // HEAD_SIZE
    group_size = query.shape[1] // (kv_heads * HEAD_SIZE)
    factor = 1.0 / math.sqrt(HEAD_SIZE)
    q_heads = query.reshape(batch_rows, kv_heads, group_size, HEAD_SIZE)
    k_heads = keys.reshape(batch_rows, positions, kv_heads, HEAD_SIZE)
    v_heads = value_rows.reshape(batch_rows, positions, kv_heads, HEAD_SIZE)
    new_keys = key_new.reshape(batch_rows, kv_heads, HEAD_SIZE)
    new_values = value_new.reshape(batch_rows, kv_heads, HEAD_SIZE).astype(jnp.float32)
    scores = (
        jnp.einsum("nhgd,nthd->nhgt", q_heads, k_heads, preferred_element_type=jnp.float32) * factor
    )
    fresh = (
        jnp.einsum("nhgd,nhd->nhg", q_heads, new_keys, preferred_element_type=jnp.float32) * factor
    )
    valid = (jnp.arange(positions, dtype=jnp.int32)[None, :] < lengths_now[:, None])[
        :, None, None, :
    ]
    peak = jnp.maximum(jnp.max(jnp.where(valid, scores, -1e30), axis=-1), fresh)
    raised = jnp.where(valid, jnp.exp(scores - peak[..., None]), 0.0)
    raised_new = jnp.exp(fresh - peak)
    total = jnp.sum(raised, axis=-1) + raised_new
    weights = (raised / total[..., None]).astype(jnp.bfloat16)
    weight_new = (raised_new / total).astype(jnp.bfloat16)
    mixed = jnp.einsum("nhgt,nthd->nhgd", weights, v_heads, preferred_element_type=jnp.float32)
    mixed = mixed + weight_new.astype(jnp.float32)[..., None] * new_values[:, :, None, :]
    return mixed.reshape(batch_rows, -1).astype(jnp.bfloat16)


def pick_sum(indicator_matrix, every):
    return jnp.sum(indicator_matrix[:, :, None] * every, axis=1)


def rank_total(partial_rows):
    return lax.psum(partial_rows, "tp").astype(jnp.bfloat16)


def adapter_row_ids(shrunk_part, base_rows, up_factor, indicator_matrix):
    every = jnp.einsum("rk,akc->rac", shrunk_part, up_factor, preferred_element_type=jnp.float32)
    return (base_rows.astype(jnp.float32) + pick_sum(indicator_matrix, every)).astype(jnp.bfloat16)


def adapt_all(
    hidden,
    base_query_proj,
    base_key_proj,
    base_value_proj,
    adapter_down_factors,
    adapter_up_query,
    adapter_up_key_value,
    indicator_matrix,
    rank_extent,
):
    every = jnp.einsum(
        "wb,xbm->wxm", hidden, adapter_down_factors, preferred_element_type=jnp.float32
    )
    shrunk = rank_total(pick_sum(indicator_matrix, every))
    query = adapter_row_ids(
        shrunk[:, :rank_extent], base_query_proj, adapter_up_query, indicator_matrix
    )
    key_new = adapter_row_ids(
        shrunk[:, rank_extent : 2 * rank_extent],
        base_key_proj,
        adapter_up_key_value[:, 0],
        indicator_matrix,
    )
    value_new = adapter_row_ids(
        shrunk[:, 2 * rank_extent :], base_value_proj, adapter_up_key_value[:, 1], indicator_matrix
    )
    return (query, key_new, value_new)


def pick(array, at):
    return lax.dynamic_index_in_dim(array, at, 0, keepdims=False)


def found(values, table):
    at = jnp.int32(0)
    for i, entry in enumerate(table):
        hit = values[0] == entry[0]
        for value, wanted in zip(values[1:], entry[1:]):
            hit = jnp.logical_and(hit, value == wanted)
        at = at + jnp.where(hit, i, 0)
    return at


def gather_kernel(
    table, stay, offset_any, resident_any, ids_any, down_any, upq_any, meta_ref, *rest
):
    packs, (offset_ref, resident_ref, ids_ref, down_ref, upq_ref, sems) = rest[:-6], rest[-6:]
    moving = len(packs)
    loads = [
        pltpu.make_async_copy(source, goal, sems.at[i])
        for i, (source, goal) in enumerate(
            (
                (offset_any, offset_ref),
                (resident_any, resident_ref),
                (ids_any, ids_ref),
                (down_any, down_ref),
                (upq_any, upq_ref),
            )
        )
    ]
    for load in loads:
        load.start()
    for load in loads[:3]:
        load.wait()
    me = lax.axis_index("rep")
    offset = [offset_ref[m] for m in range(moving)]
    place = [
        sum((offset[k] < offset[m]).astype(jnp.int32) for k in range(moving) if k != m)
        for m in range(moving)
    ]
    slot_at = [sum(jnp.where(place[m] == p, m, 0) for m in range(moving)) for p in range(moving)]
    split = down_ref.shape[1]
    pairs = []
    for p in range(moving):
        mine = ids_ref[stay + slot_at[p]]
        loaded = sum(
            jnp.where(resident_ref[n, me] == mine, n, 0) for n in range(resident_ref.shape[0])
        )
        meta_ref[2 + p] = slot_at[p]
        pairs.append((down_ref.at[loaded], packs[p].at[pl.ds(0, split)]))
        pairs.append((upq_ref.at[loaded], packs[p].at[pl.ds(split, upq_ref.shape[1])]))
    copies = [
        pltpu.make_async_copy(src, dst, sems.at[len(loads) + i])
        for i, (src, dst) in enumerate(pairs)
    ]
    for load in loads[3:]:
        load.wait()
    for copy in copies:
        copy.start()
    offset_at = [
        sum(jnp.where(place[m] == p, offset[m], 0) for m in range(moving)) for p in range(moving)
    ]
    meta_ref[0] = found(offset_at, table)
    meta_ref[1] = found(slot_at, list(itertools.permutations(range(moving))))
    for copy in copies:
        copy.wait()


def place_kernel(splits, pieces, meta_ref, *rest):
    packs, outs, sems = rest[: len(pieces)], rest[len(pieces) : -1], rest[-1]
    pool, copies = lax.axis_index("pool"), []
    for pack, (place, first_row, rows, pools) in zip(packs, pieces):
        slot = meta_ref[2 + place]
        start = 0
        for out, wanted in zip(outs, splits):
            first, last = max(start, first_row), min(start + wanted, first_row + rows)
            if first < last:
                copy = pltpu.make_async_copy(
                    pack.at[pl.ds(first - first_row, last - first)],
                    out.at[slot, pl.ds(first - start, last - first)],
                    sems.at[len(copies)],
                )
                copies.append((copy, pools))
            start += wanted

    def each(act):
        for copy, pools in copies:
            if pools is None:
                act(copy)
            else:
                pl.when(sum((pool == q).astype(jnp.int32) for q in pools) > 0)(
                    functools.partial(act, copy)
                )

    each(lambda copy: copy.start())
    each(lambda copy: copy.wait())


def place_packs(meta, moving, pieces, splits):
    arrays = [piece[0] for piece in pieces]
    width = arrays[0].shape[1]
    where = tuple((place, first, array.shape[0], pools) for array, place, first, pools in pieces)
    return pl.pallas_call(
        functools.partial(place_kernel, splits, where),
        out_shape=[
            jax.ShapeDtypeStruct((moving, rows, width), arrays[0].dtype) for rows in splits
        ],
        in_specs=[pl.BlockSpec(memory_space=pltpu.SMEM)]
        + [pl.BlockSpec(memory_space=pltpu.VMEM)] * len(arrays),
        out_specs=[pl.BlockSpec(memory_space=pltpu.HBM)] * len(splits),
        scratch_shapes=[pltpu.SemaphoreType.DMA((len(arrays) * len(splits),))],
        compiler_params=pltpu.CompilerParams(vmem_limit_bytes=KERNEL_VMEM),
        cost_estimate=pl.CostEstimate(
            flops=0, bytes_accessed=4 * moving * sum(splits) * width, transcendentals=0
        ),
    )(meta, *arrays)


def joint_kernel(table, meta_ref, other_ref, joint_ref):
    moving = other_ref.shape[0]
    own = meta_ref[0]
    other = jnp.int32(0)
    for i, entry in enumerate(table):
        hits = sum(
            (other_ref[m] == by).astype(jnp.int32) for m in range(moving) for by in entry
        )
        other = other + jnp.where(hits == moving, i, 0)
    size = len(table)
    first = lax.axis_index("pool") == 0
    joint_ref[0] = jnp.where(first, own * size + other, other * size + own)


def distance(shift, replicas):
    return min(shift % replicas, -shift % replicas)


def local(
    hidden,
    base_query_proj,
    base_key_proj,
    base_value_proj,
    key_cache,
    value_cache,
    lengths,
    adapter_down_factors,
    adapter_up_query,
    adapter_up_key_value,
    resident,
    request_adapter_id,
    migration_offset,
):
    count, model_part = hidden.shape
    moving = migration_offset.shape[0]
    stay = count - moving
    rank_extent, query_part = adapter_up_query.shape[1:]
    rank_rows = adapter_down_factors.shape[2]
    positions, kv_width = key_cache.shape[1:]
    replicas = lax.axis_size("rep")
    me = lax.axis_index("rep")
    table = list(itertools.combinations(range(1, replicas), moving))
    pools = lax.axis_size("pool")
    joint = pools == 2 and moving == 2 and len(table) <= MOST_PAIRS

    pack_rows = rank_rows + rank_extent
    cache_rows = 2 * positions + 2 * rank_extent + -(-model_part // (16 * kv_width)) * 16
    row_rows = -(-model_part // (16 * kv_width)) * 16
    small = (migration_offset, resident.T, request_adapter_id)
    factors = (jnp.swapaxes(adapter_down_factors, 1, 2), adapter_up_query)
    meta, *factor_packs = pl.pallas_call(
        functools.partial(gather_kernel, table if joint else [], stay),
        out_shape=[jax.ShapeDtypeStruct((2 + moving,), jnp.int32)]
        + [jax.ShapeDtypeStruct((pack_rows, query_part), hidden.dtype)] * moving,
        in_specs=[pl.BlockSpec(memory_space=pl.ANY)] * 5,
        out_specs=[pl.BlockSpec(memory_space=pltpu.SMEM)]
        + [pl.BlockSpec(memory_space=pltpu.HBM)] * moving,
        scratch_shapes=[pltpu.SMEM(array.shape, array.dtype) for array in small]
        + [pltpu.VMEM(array.shape, array.dtype) for array in factors]
        + [pltpu.SemaphoreType.DMA((5 + 2 * moving,))],
        compiler_params=pltpu.CompilerParams(vmem_limit_bytes=KERNEL_VMEM),
        cost_estimate=pl.CostEstimate(
            flops=0, bytes_accessed=4 * moving * pack_rows * query_part, transcendentals=0
        ),
    )(*small, *factors)

    def compute(slots):
        res_row = pick(resident, me)
        indicator_matrix = (request_adapter_id[:, None] == res_row[None, :]).astype(jnp.float32)
        own_lengths = lax.dynamic_slice_in_dim(lengths, me * count, count)
        query, key_new, value_new = adapt_all(
            hidden,
            base_query_proj,
            base_key_proj,
            base_value_proj,
            adapter_down_factors,
            adapter_up_query,
            adapter_up_key_value,
            indicator_matrix,
            rank_extent,
        )
        completed = attend(query, key_cache, value_cache, key_new, value_new, own_lengths)
        packs = []
        for slot in slots:
            row = stay + slot
            at = (jnp.arange(positions, dtype=jnp.int32) == own_lengths[row])[:, None]
            up_pair = sum(
                jnp.where(indicator_matrix[row, n] == 1, adapter_up_key_value[n], 0)
                for n in range(res_row.shape[0])
            )
            packs.append(
                jnp.concatenate(
                    [
                        jnp.where(at, key_new[row][None, :], key_cache[row]),
                        jnp.where(at, value_new[row][None, :], value_cache[row]),
                        up_pair.reshape(-1, kv_width),
                        jnp.pad(
                            completed[row].reshape(-1, kv_width),
                            ((0, row_rows - model_part // kv_width), (0, 0)),
                        ),
                    ]
                )
            )
        return (completed, *packs)

    def compute_now():
        orders = itertools.permutations(range(moving))
        return lax.switch(meta[1], [functools.partial(compute, slots) for slots in orders])

    def assemble(completed, cache_pieces, factor_pieces):
        down, upq = place_packs(meta, moving, factor_pieces, (rank_rows, rank_extent))
        slots, down, upq = lax.optimization_barrier((meta, down, upq))
        keys, value_rows, up_pair, came = place_packs(
            slots, moving, cache_pieces, (positions, positions, 2 * rank_extent, row_rows)
        )
        rows = came.reshape(moving, -1)[:, :model_part]
        return (
            jnp.concatenate([completed[:stay], rows], axis=0),
            keys,
            value_rows,
            jnp.swapaxes(down, 1, 2),
            upq,
            up_pair.reshape(moving, 2, rank_extent, kv_width),
        )

    if joint:
        first_hop = (1, -1)
        halfway = [shifted(factor_packs[p], "rep", first_hop[p]) for p in range(moving)]
        other_offset = lax.ppermute(migration_offset, "pool", [(0, 1), (1, 0)])
        chosen = pl.pallas_call(
            functools.partial(joint_kernel, table),
            out_shape=jax.ShapeDtypeStruct((1,), jnp.int32),
            in_specs=[pl.BlockSpec(memory_space=pltpu.SMEM)] * 2,
            out_specs=pl.BlockSpec(memory_space=pltpu.SMEM),
            compiler_params=pltpu.CompilerParams(vmem_limit_bytes=KERNEL_VMEM),
        )(meta, other_offset)
        completed, *cache_packs = compute_now()

        def sent(array, routes):
            pairs = [
                (start * replicas + r, end * replicas + (r + shift) % replicas)
                for start, end, shift in routes
                for r in range(replicas)
            ]
            return lax.ppermute(array, ("pool", "rep"), pairs)

        def branch(by):
            left = [[(by[q][p] - first_hop[p]) % replicas for p in range(moving)] for q in (0, 1)]
            loads = [
                sum(
                    distance(by[q][p], replicas) * cache_rows * kv_width
                    + distance(left[q][p], replicas) * pack_rows * query_part
                    for p in range(moving)
                )
                for q in (0, 1)
            ]
            slow = loads.index(max(loads))
            fast = 1 - slow
            hops = [distance(shift, replicas) for shift in by[slow]]
            far = hops.index(max(hops))
            share = (loads[slow] - loads[fast]) / (2 * hops[far] * kv_width)
            relayed = min(int(share) // 16 * 16, cache_rows - 16)
            kept = cache_rows - relayed

            def run():
                factor_pieces, cache_pieces = [], []
                for p in range(moving):
                    going = [q for q in (0, 1) if left[q][p] != 0]
                    if going:
                        hop = sent(halfway[p], [(q, q, left[q][p]) for q in going])
                        factor_pieces.append((hop, p, 0, going))
                    there = [q for q in (0, 1) if q not in going]
                    if there:
                        factor_pieces.append((halfway[p], p, 0, there))
                    whole = cache_packs[p]
                    own_way = [(q, q, by[q][p]) for q in (0, 1)]
                    if p == far and relayed:
                        part = whole[kept:]
                        across = sent(part, [(slow, fast, 0)])
                        cache_pieces.append((sent(whole[:kept], own_way), p, 0, None))
                        direct = sent(part, [(fast, fast, by[fast][p])])
                        cache_pieces.append((direct, p, kept, [fast]))
                        round_about = sent(across, [(fast, slow, by[slow][p])])
                        cache_pieces.append((round_about, p, kept, [slow]))
                    else:
                        cache_pieces.append((sent(whole, own_way), p, 0, None))
                return assemble(completed, cache_pieces, factor_pieces)

            return run

        return lax.switch(
            chosen[0], [branch(by) for by in itertools.product(table, repeat=pools)]
        )

    completed, *packs = compute_now()
    caches, factors = [], []
    for p in range(moving):
        payload = (packs[p], factor_packs[p])
        by_now = pick(migration_offset, meta[2 + p])
        for level in range((replicas - 1).bit_length()):
            payload = lax.cond(
                jnp.right_shift(by_now, level) % 2 == 1,
                lambda parts, by=1 << level: tuple(shifted(part, "rep", by) for part in parts),
                lambda parts: parts,
                payload,
            )
        caches.append(payload[0])
        factors.append(payload[1])
    return assemble(
        completed,
        [(pack, p, 0, None) for p, pack in enumerate(caches)],
        [(pack, p, 0, None) for p, pack in enumerate(factors)],
    )


def solution(mesh):
    placed = (
        P(("pool", "rep"), "tp"),
        P(("pool", "rep"), "tp"),
        P(("pool", "rep"), "tp"),
        P(("pool", "rep"), "tp"),
        P(("pool", "rep"), None, "tp"),
        P(("pool", "rep"), None, "tp"),
        P("pool"),
        P(("pool", "rep"), "tp", None),
        P(("pool", "rep"), None, "tp"),
        P(("pool", "rep"), None, None, "tp"),
        P("pool", None),
        P(("pool", "rep")),
        P("pool"),
    )
    return jax.shard_map(
        local,
        mesh=mesh,
        in_specs=placed,
        out_specs=(
            P(("pool", "rep"), "tp"),
            P(("pool", "rep"), None, "tp"),
            P(("pool", "rep"), None, "tp"),
            P(("pool", "rep"), "tp", None),
            P(("pool", "rep"), None, "tp"),
            P(("pool", "rep"), None, None, "tp"),
        ),
        check_vma=False,
    )
```

```python
import functools
import itertools
import math

import jax
import jax.numpy as jnp
from jax import lax
from jax.experimental import pallas as pl
from jax.experimental.pallas import tpu as pltpu
from jax.sharding import PartitionSpec as P

HEAD_SIZE = 128
MOST_PAIRS = 6
KERNEL_VMEM = 8 << 20


def shifted(shard, axis, by):
    size = lax.axis_size(axis)
    return lax.ppermute(shard, axis, [(i, (i + by) % size) for i in range(size)])


def attend(query, keys, value_rows, key_new, value_new, lengths_now):
    batch_rows = query.shape[0]
    positions = keys.shape[1]
    kv_heads = key_new.shape[1] // HEAD_SIZE
    group_size = query.shape[1] // (kv_heads * HEAD_SIZE)
    factor = 1.0 / math.sqrt(HEAD_SIZE)
    q_heads = query.reshape(batch_rows, kv_heads, group_size, HEAD_SIZE)
    k_heads = keys.reshape(batch_rows, positions, kv_heads, HEAD_SIZE)
    v_heads = value_rows.reshape(batch_rows, positions, kv_heads, HEAD_SIZE)
    new_keys = key_new.reshape(batch_rows, kv_heads, HEAD_SIZE)
    new_values = value_new.reshape(batch_rows, kv_heads, HEAD_SIZE).astype(jnp.float32)
    scores = (
        jnp.einsum("nhgd,nthd->nhgt", q_heads, k_heads, preferred_element_type=jnp.float32) * factor
    )
    fresh = (
        jnp.einsum("nhgd,nhd->nhg", q_heads, new_keys, preferred_element_type=jnp.float32) * factor
    )
    valid = (jnp.arange(positions, dtype=jnp.int32)[None, :] < lengths_now[:, None])[
        :, None, None, :
    ]
    peak = jnp.maximum(jnp.max(jnp.where(valid, scores, -1e30), axis=-1), fresh)
    raised = jnp.where(valid, jnp.exp(scores - peak[..., None]), 0.0)
    raised_new = jnp.exp(fresh - peak)
    total = jnp.sum(raised, axis=-1) + raised_new
    weights = (raised / total[..., None]).astype(jnp.bfloat16)
    weight_new = (raised_new / total).astype(jnp.bfloat16)
    mixed = jnp.einsum("nhgt,nthd->nhgd", weights, v_heads, preferred_element_type=jnp.float32)
    mixed = mixed + weight_new.astype(jnp.float32)[..., None] * new_values[:, :, None, :]
    return mixed.reshape(batch_rows, -1).astype(jnp.bfloat16)


def pick_sum(indicator_matrix, every):
    return jnp.sum(indicator_matrix[:, :, None] * every, axis=1)


def rank_total(partial_rows):
    return lax.psum(partial_rows, "tp").astype(jnp.bfloat16)


def adapter_row_ids(shrunk_part, base_rows, up_factor, indicator_matrix):
    every = jnp.einsum("rk,akc->rac", shrunk_part, up_factor, preferred_element_type=jnp.float32)
    return (base_rows.astype(jnp.float32) + pick_sum(indicator_matrix, every)).astype(jnp.bfloat16)


def adapt_all(
    hidden,
    base_query_proj,
    base_key_proj,
    base_value_proj,
    adapter_down_factors,
    adapter_up_query,
    adapter_up_key_value,
    indicator_matrix,
    rank_extent,
):
    every = jnp.einsum(
        "wb,xbm->wxm", hidden, adapter_down_factors, preferred_element_type=jnp.float32
    )
    shrunk = rank_total(pick_sum(indicator_matrix, every))
    query = adapter_row_ids(
        shrunk[:, :rank_extent], base_query_proj, adapter_up_query, indicator_matrix
    )
    key_new = adapter_row_ids(
        shrunk[:, rank_extent : 2 * rank_extent],
        base_key_proj,
        adapter_up_key_value[:, 0],
        indicator_matrix,
    )
    value_new = adapter_row_ids(
        shrunk[:, 2 * rank_extent :], base_value_proj, adapter_up_key_value[:, 1], indicator_matrix
    )
    return (query, key_new, value_new)


def pick(array, at):
    return lax.dynamic_index_in_dim(array, at, 0, keepdims=False)


def found(values, table):
    at = jnp.int32(0)
    for i, entry in enumerate(table):
        hit = values[0] == entry[0]
        for value, wanted in zip(values[1:], entry[1:]):
            hit = jnp.logical_and(hit, value == wanted)
        at = at + jnp.where(hit, i, 0)
    return at


def gather_kernel(
    table, stay, offset_any, resident_any, ids_any, down_any, upq_any, meta_ref, *rest
):
    packs, (offset_ref, resident_ref, ids_ref, down_ref, upq_ref, sems) = rest[:-6], rest[-6:]
    moving = len(packs)
    loads = [
        pltpu.make_async_copy(source, goal, sems.at[i])
        for i, (source, goal) in enumerate(
            (
                (offset_any, offset_ref),
                (resident_any, resident_ref),
                (ids_any, ids_ref),
                (down_any, down_ref),
                (upq_any, upq_ref),
            )
        )
    ]
    for load in loads:
        load.start()
    for load in loads[:3]:
        load.wait()
    me = lax.axis_index("rep")
    offset = [offset_ref[m] for m in range(moving)]
    place = [
        sum((offset[k] < offset[m]).astype(jnp.int32) for k in range(moving) if k != m)
        for m in range(moving)
    ]
    slot_at = [sum(jnp.where(place[m] == p, m, 0) for m in range(moving)) for p in range(moving)]
    split = down_ref.shape[1]
    pairs = []
    for p in range(moving):
        mine = ids_ref[stay + slot_at[p]]
        loaded = sum(
            jnp.where(resident_ref[n, me] == mine, n, 0) for n in range(resident_ref.shape[0])
        )
        meta_ref[2 + p] = slot_at[p]
        pairs.append((down_ref.at[loaded], packs[p].at[pl.ds(0, split)]))
        pairs.append((upq_ref.at[loaded], packs[p].at[pl.ds(split, upq_ref.shape[1])]))
    copies = [
        pltpu.make_async_copy(src, dst, sems.at[len(loads) + i])
        for i, (src, dst) in enumerate(pairs)
    ]
    for load in loads[3:]:
        load.wait()
    for copy in copies:
        copy.start()
    offset_at = [
        sum(jnp.where(place[m] == p, offset[m], 0) for m in range(moving)) for p in range(moving)
    ]
    meta_ref[0] = found(offset_at, table)
    meta_ref[1] = found(slot_at, list(itertools.permutations(range(moving))))
    for copy in copies:
        copy.wait()


def place_kernel(splits, pieces, row_arrays, stay, meta_ref, *rest):
    packs, rest, sems = rest[: len(pieces)], rest[len(pieces) : -1], rest[-1]
    if row_arrays:
        rows_in, rows_out, rows_now = rest[0], rest[-2], rest[-1]
        rest = rest[1:-2]
    outs = rest[-len(splits) :]
    pool, copies = lax.axis_index("pool"), []
    for pack, (place, first_row, rows, pools) in zip(packs, pieces):
        slot = meta_ref[2 + place]
        start = 0
        for out, wanted in zip(outs, splits):
            first, last = max(start, first_row), min(start + wanted, first_row + rows)
            if first < last:
                copy = pltpu.make_async_copy(
                    pack.at[pl.ds(first - first_row, last - first)],
                    out.at[slot, pl.ds(first - start, last - first)],
                    sems.at[len(copies)],
                )
                copies.append((copy, pools))
            start += wanted

    def in_pools(pools):
        return sum((pool == q).astype(jnp.int32) for q in pools) > 0

    def each(act):
        for copy, pools in copies:
            if pools is None:
                act(copy)
            else:
                pl.when(in_pools(pools))(functools.partial(act, copy))

    each(lambda copy: copy.start())
    if row_arrays:
        now = rows_in[...].astype(jnp.float32)
        at = lax.broadcasted_iota(jnp.int32, now.shape, 0)
        for place, holders in row_arrays:
            row = None
            for i in holders:
                tail = packs[i][pl.ds(packs[i].shape[0] - 16, 16), :].astype(jnp.float32)
                parts = now.shape[1] // tail.shape[1]
                flat = jnp.concatenate([tail[c : c + 1] for c in range(parts)], axis=1)
                row = flat if row is None else jnp.where(in_pools(pieces[i][3]), flat, row)
            now = jnp.where(at == stay + meta_ref[2 + place], row, now)
        rows_now[...] = now.astype(rows_now.dtype)
        leaving = pltpu.make_async_copy(rows_now, rows_out, sems.at[len(copies)])
        leaving.start()
        leaving.wait()
    each(lambda copy: copy.wait())


def place_packs(meta, moving, pieces, splits, attended=None, into=None):
    arrays = [piece[0] for piece in pieces]
    width = arrays[0].shape[1]
    where = tuple((place, first, array.shape[0], pools) for array, place, first, pools in pieces)
    vmem, hbm = (pl.BlockSpec(memory_space=space) for space in (pltpu.VMEM, pltpu.HBM))
    out_shape = [jax.ShapeDtypeStruct((moving, rows, width), arrays[0].dtype) for rows in splits]
    in_specs = [pl.BlockSpec(memory_space=pltpu.SMEM)] + [vmem] * len(arrays)
    scratch = [pltpu.SemaphoreType.DMA((len(pieces) * len(splits) + 1,))]
    row_arrays, stay = None, None
    if attended is not None:
        end = max(first + rows for _, first, rows, _ in where)
        row_arrays = [
            (p, [i for i, (at, first, rows, _) in enumerate(where) if at == p and first + rows == end])
            for p in sorted({place for place, _, _, _ in where})
        ]
        stay = attended.shape[0] - moving
        arrays.append(attended)
        in_specs.append(vmem)
        out_shape.append(jax.ShapeDtypeStruct(attended.shape, attended.dtype))
        scratch.insert(0, pltpu.VMEM(attended.shape, attended.dtype))
    aliases = {}
    if into is not None:
        aliases = {1 + len(arrays) + i: i for i in range(len(splits))}
        arrays = arrays + list(into)
        in_specs = in_specs + [hbm] * len(splits)
    return pl.pallas_call(
        functools.partial(place_kernel, splits, where, row_arrays, stay),
        out_shape=out_shape,
        in_specs=in_specs,
        out_specs=[hbm] * len(out_shape),
        scratch_shapes=scratch,
        input_output_aliases=aliases,
        compiler_params=pltpu.CompilerParams(vmem_limit_bytes=KERNEL_VMEM),
        cost_estimate=pl.CostEstimate(
            flops=0, bytes_accessed=4 * sum(array.size for array in arrays), transcendentals=0
        ),
    )(meta, *arrays)


def joint_kernel(table, meta_ref, other_ref, joint_ref):
    moving = other_ref.shape[0]
    own = meta_ref[0]
    other = jnp.int32(0)
    for i, entry in enumerate(table):
        hits = sum(
            (other_ref[m] == by).astype(jnp.int32) for m in range(moving) for by in entry
        )
        other = other + jnp.where(hits == moving, i, 0)
    size = len(table)
    first = lax.axis_index("pool") == 0
    joint_ref[0] = jnp.where(first, own * size + other, other * size + own)


def distance(shift, replicas):
    return min(shift % replicas, -shift % replicas)


def local(
    hidden,
    base_query_proj,
    base_key_proj,
    base_value_proj,
    key_cache,
    value_cache,
    lengths,
    adapter_down_factors,
    adapter_up_query,
    adapter_up_key_value,
    resident,
    request_adapter_id,
    migration_offset,
):
    count, model_part = hidden.shape
    moving = migration_offset.shape[0]
    stay = count - moving
    rank_extent, query_part = adapter_up_query.shape[1:]
    rank_rows = adapter_down_factors.shape[2]
    positions, kv_width = key_cache.shape[1:]
    replicas = lax.axis_size("rep")
    me = lax.axis_index("rep")
    table = list(itertools.combinations(range(1, replicas), moving))
    pools = lax.axis_size("pool")
    joint = pools == 2 and moving == 2 and len(table) <= MOST_PAIRS

    pack_rows = rank_rows + rank_extent
    cache_rows = 2 * positions + 2 * rank_extent + -(-model_part // (16 * kv_width)) * 16
    row_rows = -(-model_part // (16 * kv_width)) * 16
    small = (migration_offset, resident.T, request_adapter_id)
    factors = (jnp.swapaxes(adapter_down_factors, 1, 2), adapter_up_query)
    meta, *factor_packs = pl.pallas_call(
        functools.partial(gather_kernel, table if joint else [], stay),
        out_shape=[jax.ShapeDtypeStruct((2 + moving,), jnp.int32)]
        + [jax.ShapeDtypeStruct((pack_rows, query_part), hidden.dtype)] * moving,
        in_specs=[pl.BlockSpec(memory_space=pl.ANY)] * 5,
        out_specs=[pl.BlockSpec(memory_space=pltpu.SMEM)]
        + [pl.BlockSpec(memory_space=pltpu.HBM)] * moving,
        scratch_shapes=[pltpu.SMEM(array.shape, array.dtype) for array in small]
        + [pltpu.VMEM(array.shape, array.dtype) for array in factors]
        + [pltpu.SemaphoreType.DMA((5 + 2 * moving,))],
        compiler_params=pltpu.CompilerParams(vmem_limit_bytes=KERNEL_VMEM),
        cost_estimate=pl.CostEstimate(
            flops=0, bytes_accessed=4 * moving * pack_rows * query_part, transcendentals=0
        ),
    )(*small, *factors)

    def compute(slots):
        res_row = pick(resident, me)
        indicator_matrix = (request_adapter_id[:, None] == res_row[None, :]).astype(jnp.float32)
        own_lengths = lax.dynamic_slice_in_dim(lengths, me * count, count)
        query, key_new, value_new = adapt_all(
            hidden,
            base_query_proj,
            base_key_proj,
            base_value_proj,
            adapter_down_factors,
            adapter_up_query,
            adapter_up_key_value,
            indicator_matrix,
            rank_extent,
        )
        completed = attend(query, key_cache, value_cache, key_new, value_new, own_lengths)
        packs = []
        for slot in slots:
            row = stay + slot
            at = (jnp.arange(positions, dtype=jnp.int32) == own_lengths[row])[:, None]
            up_pair = sum(
                jnp.where(indicator_matrix[row, n] == 1, adapter_up_key_value[n], 0)
                for n in range(res_row.shape[0])
            )
            packs.append(
                jnp.concatenate(
                    [
                        jnp.where(at, key_new[row][None, :], key_cache[row]),
                        jnp.where(at, value_new[row][None, :], value_cache[row]),
                        up_pair.reshape(-1, kv_width),
                        jnp.pad(
                            completed[row].reshape(-1, kv_width),
                            ((0, row_rows - model_part // kv_width), (0, 0)),
                        ),
                    ]
                )
            )
        return (completed, *packs)

    def compute_now():
        orders = itertools.permutations(range(moving))
        return lax.switch(meta[1], [functools.partial(compute, slots) for slots in orders])

    def assemble(completed, cache_pieces, factor_pieces, last=moving - 1):
        down, upq = place_packs(meta, moving, factor_pieces, (rank_rows, rank_extent))
        cache_parts = (positions, positions, 2 * rank_extent)
        attended, into = completed, None
        for p in [p for p in range(moving) if p != last] + [last]:
            slots, attended, into, (down, upq) = lax.optimization_barrier(
                (meta, attended, into, (down, upq))
            )
            mine = [piece for piece in cache_pieces if piece[1] == p]
            *into, attended = place_packs(slots, moving, mine, cache_parts, attended, into)
        keys, value_rows, up_pair = into
        return (
            attended,
            keys,
            value_rows,
            jnp.swapaxes(down, 1, 2),
            upq,
            up_pair.reshape(moving, 2, rank_extent, kv_width),
        )

    if joint:
        first_hop = (1, -1)
        halfway = [shifted(factor_packs[p], "rep", first_hop[p]) for p in range(moving)]
        other_offset = lax.ppermute(migration_offset, "pool", [(0, 1), (1, 0)])
        chosen = pl.pallas_call(
            functools.partial(joint_kernel, table),
            out_shape=jax.ShapeDtypeStruct((1,), jnp.int32),
            in_specs=[pl.BlockSpec(memory_space=pltpu.SMEM)] * 2,
            out_specs=pl.BlockSpec(memory_space=pltpu.SMEM),
            compiler_params=pltpu.CompilerParams(vmem_limit_bytes=KERNEL_VMEM),
        )(meta, other_offset)
        completed, *cache_packs = compute_now()

        def sent(array, routes):
            pairs = [
                (start * replicas + r, end * replicas + (r + shift) % replicas)
                for start, end, shift in routes
                for r in range(replicas)
            ]
            return lax.ppermute(array, ("pool", "rep"), pairs)

        def branch(by):
            left = [[(by[q][p] - first_hop[p]) % replicas for p in range(moving)] for q in (0, 1)]
            loads = [
                sum(
                    distance(by[q][p], replicas) * cache_rows * kv_width
                    + distance(left[q][p], replicas) * pack_rows * query_part
                    for p in range(moving)
                )
                for q in (0, 1)
            ]
            slow = loads.index(max(loads))
            fast = 1 - slow
            hops = [distance(shift, replicas) for shift in by[slow]]
            far = hops.index(max(hops))
            share = (loads[slow] - loads[fast]) / (2 * hops[far] * kv_width)
            relayed = min(int(share) // 16 * 16, cache_rows - 16)
            kept = cache_rows - relayed

            def run():
                factor_pieces, cache_pieces = [], []
                for p in range(moving):
                    going = [q for q in (0, 1) if left[q][p] != 0]
                    if going:
                        hop = sent(halfway[p], [(q, q, left[q][p]) for q in going])
                        factor_pieces.append((hop, p, 0, going))
                    there = [q for q in (0, 1) if q not in going]
                    if there:
                        factor_pieces.append((halfway[p], p, 0, there))
                    whole = cache_packs[p]
                    own_way = [(q, q, by[q][p]) for q in (0, 1)]
                    if p == far and relayed:
                        part = whole[kept:]
                        across = sent(part, [(slow, fast, 0)])
                        cache_pieces.append((sent(whole[:kept], own_way), p, 0, None))
                        direct = sent(part, [(fast, fast, by[fast][p])])
                        cache_pieces.append((direct, p, kept, [fast]))
                        round_about = sent(across, [(fast, slow, by[slow][p])])
                        cache_pieces.append((round_about, p, kept, [slow]))
                    else:
                        cache_pieces.append((sent(whole, own_way), p, 0, None))
                return assemble(completed, cache_pieces, factor_pieces, far)

            return run

        return lax.switch(
            chosen[0], [branch(by) for by in itertools.product(table, repeat=pools)]
        )

    completed, *packs = compute_now()
    caches, factors = [], []
    for p in range(moving):
        payload = (packs[p], factor_packs[p])
        by_now = pick(migration_offset, meta[2 + p])
        for level in range((replicas - 1).bit_length()):
            payload = lax.cond(
                jnp.right_shift(by_now, level) % 2 == 1,
                lambda parts, by=1 << level: tuple(shifted(part, "rep", by) for part in parts),
                lambda parts: parts,
                payload,
            )
        caches.append(payload[0])
        factors.append(payload[1])
    return assemble(
        completed,
        [(pack, p, 0, None) for p, pack in enumerate(caches)],
        [(pack, p, 0, None) for p, pack in enumerate(factors)],
    )


def solution(mesh):
    placed = (
        P(("pool", "rep"), "tp"),
        P(("pool", "rep"), "tp"),
        P(("pool", "rep"), "tp"),
        P(("pool", "rep"), "tp"),
        P(("pool", "rep"), None, "tp"),
        P(("pool", "rep"), None, "tp"),
        P("pool"),
        P(("pool", "rep"), "tp", None),
        P(("pool", "rep"), None, "tp"),
        P(("pool", "rep"), None, None, "tp"),
        P("pool", None),
        P(("pool", "rep")),
        P("pool"),
    )
    return jax.shard_map(
        local,
        mesh=mesh,
        in_specs=placed,
        out_specs=(
            P(("pool", "rep"), "tp"),
            P(("pool", "rep"), None, "tp"),
            P(("pool", "rep"), None, "tp"),
            P(("pool", "rep"), "tp", None),
            P(("pool", "rep"), None, "tp"),
            P(("pool", "rep"), None, None, "tp"),
        ),
        check_vma=False,
    )
```

```python
import functools
import itertools
import math

import jax
import jax.numpy as jnp
from jax import lax
from jax.experimental import pallas as pl
from jax.experimental.pallas import tpu as pltpu
from jax.sharding import PartitionSpec as P

HEAD_SIZE = 128
KERNEL_VMEM = 8 << 20


def shifted(shard, axis, by):
    size = lax.axis_size(axis)
    return lax.ppermute(shard, axis, [(i, (i + by) % size) for i in range(size)])


def attend(query, keys, value_rows, key_new, value_new, lengths_now):
    batch_rows = query.shape[0]
    positions = keys.shape[1]
    kv_heads = key_new.shape[1] // HEAD_SIZE
    group_size = query.shape[1] // (kv_heads * HEAD_SIZE)
    factor = 1.0 / math.sqrt(HEAD_SIZE)
    q_heads = query.reshape(batch_rows, kv_heads, group_size, HEAD_SIZE)
    k_heads = keys.reshape(batch_rows, positions, kv_heads, HEAD_SIZE)
    v_heads = value_rows.reshape(batch_rows, positions, kv_heads, HEAD_SIZE)
    new_keys = key_new.reshape(batch_rows, kv_heads, HEAD_SIZE)
    new_values = value_new.reshape(batch_rows, kv_heads, HEAD_SIZE).astype(jnp.float32)
    scores = (
        jnp.einsum("nhgd,nthd->nhgt", q_heads, k_heads, preferred_element_type=jnp.float32) * factor
    )
    fresh = (
        jnp.einsum("nhgd,nhd->nhg", q_heads, new_keys, preferred_element_type=jnp.float32) * factor
    )
    valid = (jnp.arange(positions, dtype=jnp.int32)[None, :] < lengths_now[:, None])[
        :, None, None, :
    ]
    peak = jnp.maximum(jnp.max(jnp.where(valid, scores, -1e30), axis=-1), fresh)
    raised = jnp.where(valid, jnp.exp(scores - peak[..., None]), 0.0)
    raised_new = jnp.exp(fresh - peak)
    total = jnp.sum(raised, axis=-1) + raised_new
    weights = (raised / total[..., None]).astype(jnp.bfloat16)
    weight_new = (raised_new / total).astype(jnp.bfloat16)
    mixed = jnp.einsum("nhgt,nthd->nhgd", weights, v_heads, preferred_element_type=jnp.float32)
    mixed = mixed + weight_new.astype(jnp.float32)[..., None] * new_values[:, :, None, :]
    return mixed.reshape(batch_rows, -1).astype(jnp.bfloat16)


def pick_sum(indicator_matrix, every):
    return jnp.sum(indicator_matrix[:, :, None] * every, axis=1)


def rank_total(partial_rows):
    return lax.psum(partial_rows, "tp").astype(jnp.bfloat16)


def adapter_row_ids(shrunk_part, base_rows, up_factor, indicator_matrix):
    every = jnp.einsum("rk,akc->rac", shrunk_part, up_factor, preferred_element_type=jnp.float32)
    return (base_rows.astype(jnp.float32) + pick_sum(indicator_matrix, every)).astype(jnp.bfloat16)


def adapt_all(
    hidden,
    base_query_proj,
    base_key_proj,
    base_value_proj,
    adapter_down_factors,
    adapter_up_query,
    adapter_up_key_value,
    indicator_matrix,
    rank_extent,
):
    every = jnp.einsum(
        "wb,xbm->wxm", hidden, adapter_down_factors, preferred_element_type=jnp.float32
    )
    shrunk = rank_total(pick_sum(indicator_matrix, every))
    query = adapter_row_ids(
        shrunk[:, :rank_extent], base_query_proj, adapter_up_query, indicator_matrix
    )
    key_new = adapter_row_ids(
        shrunk[:, rank_extent : 2 * rank_extent],
        base_key_proj,
        adapter_up_key_value[:, 0],
        indicator_matrix,
    )
    value_new = adapter_row_ids(
        shrunk[:, 2 * rank_extent :], base_value_proj, adapter_up_key_value[:, 1], indicator_matrix
    )
    return (query, key_new, value_new)


def pick(array, at):
    return lax.dynamic_index_in_dim(array, at, 0, keepdims=False)


def found(values, table):
    at = jnp.int32(0)
    for i, entry in enumerate(table):
        hit = values[0] == entry[0]
        for value, wanted in zip(values[1:], entry[1:]):
            hit = jnp.logical_and(hit, value == wanted)
        at = at + jnp.where(hit, i, 0)
    return at


def gather_kernel(
    table, stay, offset_any, resident_any, ids_any, down_any, upq_any, meta_ref, *rest
):
    packs, (offset_ref, resident_ref, ids_ref, down_ref, upq_ref, sems) = rest[:-6], rest[-6:]
    moving = len(packs)
    loads = [
        pltpu.make_async_copy(source, goal, sems.at[i])
        for i, (source, goal) in enumerate(
            (
                (offset_any, offset_ref),
                (resident_any, resident_ref),
                (ids_any, ids_ref),
                (down_any, down_ref),
                (upq_any, upq_ref),
            )
        )
    ]
    for load in loads:
        load.start()
    for load in loads[:3]:
        load.wait()
    me = lax.axis_index("rep")
    offset = [offset_ref[m] for m in range(moving)]
    place = [
        sum((offset[k] < offset[m]).astype(jnp.int32) for k in range(moving) if k != m)
        for m in range(moving)
    ]
    slot_at = [sum(jnp.where(place[m] == p, m, 0) for m in range(moving)) for p in range(moving)]
    split = down_ref.shape[1]
    pairs = []
    for p in range(moving):
        mine = ids_ref[stay + slot_at[p]]
        loaded = sum(
            jnp.where(resident_ref[n, me] == mine, n, 0) for n in range(resident_ref.shape[0])
        )
        meta_ref[2 + p] = slot_at[p]
        pairs.append((down_ref.at[loaded], packs[p].at[pl.ds(0, split)]))
        pairs.append((upq_ref.at[loaded], packs[p].at[pl.ds(split, upq_ref.shape[1])]))
    copies = [
        pltpu.make_async_copy(src, dst, sems.at[len(loads) + i])
        for i, (src, dst) in enumerate(pairs)
    ]
    for load in loads[3:]:
        load.wait()
    for copy in copies:
        copy.start()
    offset_at = [
        sum(jnp.where(place[m] == p, offset[m], 0) for m in range(moving)) for p in range(moving)
    ]
    meta_ref[0] = found(offset_at, table)
    meta_ref[1] = found(slot_at, list(itertools.permutations(range(moving))))
    for copy in copies:
        copy.wait()


def place_kernel(splits, pieces, row_arrays, stay, meta_ref, *rest):
    packs, rest, sems = rest[: len(pieces)], rest[len(pieces) : -1], rest[-1]
    if row_arrays:
        rows_in, rows_out, rows_now = rest[0], rest[-2], rest[-1]
        rest = rest[1:-2]
    outs = rest[-len(splits) :]
    pool, copies = lax.axis_index("pool"), []
    for pack, (place, first_row, rows, pools) in zip(packs, pieces):
        slot = meta_ref[2 + place]
        start = 0
        for out, wanted in zip(outs, splits):
            first, last = max(start, first_row), min(start + wanted, first_row + rows)
            if first < last:
                copy = pltpu.make_async_copy(
                    pack.at[pl.ds(first - first_row, last - first)],
                    out.at[slot, pl.ds(first - start, last - first)],
                    sems.at[len(copies)],
                )
                copies.append((copy, pools))
            start += wanted

    def in_pools(pools):
        return sum((pool == q).astype(jnp.int32) for q in pools) > 0

    def each(act):
        for copy, pools in copies:
            if pools is None:
                act(copy)
            else:
                pl.when(in_pools(pools))(functools.partial(act, copy))

    each(lambda copy: copy.start())
    if row_arrays:
        now = rows_in[...].astype(jnp.float32)
        at = lax.broadcasted_iota(jnp.int32, now.shape, 0)
        for place, holders in row_arrays:
            row = None
            for i in holders:
                tail = packs[i][pl.ds(packs[i].shape[0] - 16, 16), :].astype(jnp.float32)
                parts = now.shape[1] // tail.shape[1]
                flat = jnp.concatenate([tail[c : c + 1] for c in range(parts)], axis=1)
                row = flat if row is None else jnp.where(in_pools(pieces[i][3]), flat, row)
            now = jnp.where(at == stay + meta_ref[2 + place], row, now)
        rows_now[...] = now.astype(rows_now.dtype)
        leaving = pltpu.make_async_copy(rows_now, rows_out, sems.at[len(copies)])
        leaving.start()
        leaving.wait()
    each(lambda copy: copy.wait())


def place_packs(meta, moving, pieces, splits, attended=None, into=None):
    arrays = [piece[0] for piece in pieces]
    width = arrays[0].shape[1]
    where = tuple((place, first, array.shape[0], pools) for array, place, first, pools in pieces)
    vmem, hbm = (pl.BlockSpec(memory_space=space) for space in (pltpu.VMEM, pltpu.HBM))
    out_shape = [jax.ShapeDtypeStruct((moving, rows, width), arrays[0].dtype) for rows in splits]
    in_specs = [pl.BlockSpec(memory_space=pltpu.SMEM)] + [vmem] * len(arrays)
    scratch = [pltpu.SemaphoreType.DMA((len(pieces) * len(splits) + 1,))]
    row_arrays, stay = None, None
    if attended is not None:
        end = max(first + rows for _, first, rows, _ in where)
        row_arrays = [
            (p, [i for i, (at, first, rows, _) in enumerate(where) if at == p and first + rows == end])
            for p in sorted({place for place, _, _, _ in where})
        ]
        stay = attended.shape[0] - moving
        arrays.append(attended)
        in_specs.append(vmem)
        out_shape.append(jax.ShapeDtypeStruct(attended.shape, attended.dtype))
        scratch.insert(0, pltpu.VMEM(attended.shape, attended.dtype))
    aliases = {}
    if into is not None:
        aliases = {1 + len(arrays) + i: i for i in range(len(splits))}
        arrays = arrays + list(into)
        in_specs = in_specs + [hbm] * len(splits)
    return pl.pallas_call(
        functools.partial(place_kernel, splits, where, row_arrays, stay),
        out_shape=out_shape,
        in_specs=in_specs,
        out_specs=[hbm] * len(out_shape),
        scratch_shapes=scratch,
        input_output_aliases=aliases,
        compiler_params=pltpu.CompilerParams(vmem_limit_bytes=KERNEL_VMEM),
        cost_estimate=pl.CostEstimate(
            flops=0, bytes_accessed=4 * sum(array.size for array in arrays), transcendentals=0
        ),
    )(meta, *arrays)


def joint_kernel(table, meta_ref, other_ref, joint_ref):
    moving = other_ref.shape[0]
    own = meta_ref[0]
    other = jnp.int32(0)
    for i, entry in enumerate(table):
        hits = sum(
            (other_ref[m] == by).astype(jnp.int32) for m in range(moving) for by in entry
        )
        other = other + jnp.where(hits == moving, i, 0)
    size = len(table)
    first = lax.axis_index("pool") == 0
    joint_ref[0] = jnp.where(first, own * size + other, other * size + own)


def distance(shift, replicas):
    return min(shift % replicas, -shift % replicas)


def local(
    hidden,
    base_query_proj,
    base_key_proj,
    base_value_proj,
    key_cache,
    value_cache,
    lengths,
    adapter_down_factors,
    adapter_up_query,
    adapter_up_key_value,
    resident,
    request_adapter_id,
    migration_offset,
):
    count, model_part = hidden.shape
    moving = migration_offset.shape[0]
    stay = count - moving
    rank_extent, query_part = adapter_up_query.shape[1:]
    rank_rows = adapter_down_factors.shape[2]
    positions, kv_width = key_cache.shape[1:]
    replicas = lax.axis_size("rep")
    me = lax.axis_index("rep")
    table = list(itertools.combinations(range(1, replicas), moving))
    pools = lax.axis_size("pool")
    first_hop = (1, -1)
    joint = (
        pools == 2
        and moving == 2
        and len(table) > 0
        and all(
            sum((by[p] - first_hop[p]) % replicas != 0 for p in range(moving)) <= 1
            for by in table
        )
    )

    pack_rows = rank_rows + rank_extent
    cache_rows = 2 * positions + 2 * rank_extent + -(-model_part // (16 * kv_width)) * 16
    row_rows = -(-model_part // (16 * kv_width)) * 16
    small = (migration_offset, resident.T, request_adapter_id)
    factors = (jnp.swapaxes(adapter_down_factors, 1, 2), adapter_up_query)
    meta, *factor_packs = pl.pallas_call(
        functools.partial(gather_kernel, table if joint else [], stay),
        out_shape=[jax.ShapeDtypeStruct((2 + moving,), jnp.int32)]
        + [jax.ShapeDtypeStruct((pack_rows, query_part), hidden.dtype)] * moving,
        in_specs=[pl.BlockSpec(memory_space=pl.ANY)] * 5,
        out_specs=[pl.BlockSpec(memory_space=pltpu.SMEM)]
        + [pl.BlockSpec(memory_space=pltpu.HBM)] * moving,
        scratch_shapes=[pltpu.SMEM(array.shape, array.dtype) for array in small]
        + [pltpu.VMEM(array.shape, array.dtype) for array in factors]
        + [pltpu.SemaphoreType.DMA((5 + 2 * moving,))],
        compiler_params=pltpu.CompilerParams(vmem_limit_bytes=KERNEL_VMEM),
        cost_estimate=pl.CostEstimate(
            flops=0, bytes_accessed=4 * moving * pack_rows * query_part, transcendentals=0
        ),
    )(*small, *factors)

    def compute(slots):
        res_row = pick(resident, me)
        indicator_matrix = (request_adapter_id[:, None] == res_row[None, :]).astype(jnp.float32)
        own_lengths = lax.dynamic_slice_in_dim(lengths, me * count, count)
        query, key_new, value_new = adapt_all(
            hidden,
            base_query_proj,
            base_key_proj,
            base_value_proj,
            adapter_down_factors,
            adapter_up_query,
            adapter_up_key_value,
            indicator_matrix,
            rank_extent,
        )
        completed = attend(query, key_cache, value_cache, key_new, value_new, own_lengths)
        packs = []
        for slot in slots:
            row = stay + slot
            at = (jnp.arange(positions, dtype=jnp.int32) == own_lengths[row])[:, None]
            up_pair = sum(
                jnp.where(indicator_matrix[row, n] == 1, adapter_up_key_value[n], 0)
                for n in range(res_row.shape[0])
            )
            packs.append(
                jnp.concatenate(
                    [
                        jnp.where(at, key_new[row][None, :], key_cache[row]),
                        jnp.where(at, value_new[row][None, :], value_cache[row]),
                        up_pair.reshape(-1, kv_width),
                        jnp.pad(
                            completed[row].reshape(-1, kv_width),
                            ((0, row_rows - model_part // kv_width), (0, 0)),
                        ),
                    ]
                )
            )
        return (completed, *packs)

    def compute_now():
        orders = itertools.permutations(range(moving))
        return lax.switch(meta[1], [functools.partial(compute, slots) for slots in orders])

    def assemble(completed, cache_pieces, factor_pieces, last=moving - 1):
        down, upq = place_packs(meta, moving, factor_pieces, (rank_rows, rank_extent))
        cache_parts = (positions, positions, 2 * rank_extent)
        attended, into = completed, None
        for p in [p for p in range(moving) if p != last] + [last]:
            slots, attended, into, (down, upq) = lax.optimization_barrier(
                (meta, attended, into, (down, upq))
            )
            mine = [piece for piece in cache_pieces if piece[1] == p]
            *into, attended = place_packs(slots, moving, mine, cache_parts, attended, into)
        keys, value_rows, up_pair = into
        return (
            attended,
            keys,
            value_rows,
            jnp.swapaxes(down, 1, 2),
            upq,
            up_pair.reshape(moving, 2, rank_extent, kv_width),
        )

    if joint:
        halfway = [shifted(factor_packs[p], "rep", first_hop[p]) for p in range(moving)]
        other_offset = lax.ppermute(migration_offset, "pool", [(0, 1), (1, 0)])
        chosen = pl.pallas_call(
            functools.partial(joint_kernel, table),
            out_shape=jax.ShapeDtypeStruct((1,), jnp.int32),
            in_specs=[pl.BlockSpec(memory_space=pltpu.SMEM)] * 2,
            out_specs=pl.BlockSpec(memory_space=pltpu.SMEM),
            compiler_params=pltpu.CompilerParams(vmem_limit_bytes=KERNEL_VMEM),
        )(meta, other_offset)
        completed, *cache_packs = compute_now()

        def sent(array, routes):
            pairs = [
                (start * replicas + r, end * replicas + (r + shift) % replicas)
                for start, end, shift in routes
                for r in range(replicas)
            ]
            return lax.ppermute(array, ("pool", "rep"), pairs)

        def branch(by):
            left = [[(by[q][p] - first_hop[p]) % replicas for p in range(moving)] for q in (0, 1)]
            loads = [
                sum(
                    distance(by[q][p], replicas) * cache_rows * kv_width
                    + distance(left[q][p], replicas) * pack_rows * query_part
                    for p in range(moving)
                )
                for q in (0, 1)
            ]
            slow = loads.index(max(loads))
            fast = 1 - slow
            hops = [distance(shift, replicas) for shift in by[slow]]
            far = hops.index(max(hops))
            share = (loads[slow] - loads[fast]) / (2 * hops[far] * kv_width)
            relayed = min(int(share) // 16 * 16, cache_rows - 16)
            kept = cache_rows - relayed

            def run():
                factor_pieces, cache_pieces = [], []
                going = {q: p for q in (0, 1) for p in range(moving) if left[q][p] != 0}
                if going:
                    operands = [halfway[going.get(q, going[slow])] for q in (0, 1)]
                    operand = operands[0]
                    if operands[1] is not operand:
                        operand = jnp.where(lax.axis_index("pool") == 0, *operands)
                    hop = sent(operand, [(q, q, left[q][p]) for q, p in going.items()])
                for p in range(moving):
                    there = [q for q in (0, 1) if going.get(q) == p]
                    if there:
                        factor_pieces.append((hop, p, 0, there))
                    stayed = [q for q in (0, 1) if q not in there]
                    if stayed:
                        factor_pieces.append((halfway[p], p, 0, stayed))
                    whole = cache_packs[p]
                    own_way = [(q, q, by[q][p]) for q in (0, 1)]
                    if p == far and relayed:
                        part = whole[kept:]
                        across = sent(part, [(slow, fast, 0)])
                        cache_pieces.append((sent(whole[:kept], own_way), p, 0, None))
                        direct = sent(part, [(fast, fast, by[fast][p])])
                        cache_pieces.append((direct, p, kept, [fast]))
                        round_about = sent(across, [(fast, slow, by[slow][p])])
                        cache_pieces.append((round_about, p, kept, [slow]))
                    else:
                        cache_pieces.append((sent(whole, own_way), p, 0, None))
                return assemble(completed, cache_pieces, factor_pieces, far)

            return run

        return lax.switch(
            chosen[0], [branch(by) for by in itertools.product(table, repeat=pools)]
        )

    completed, *packs = compute_now()
    caches, factors = [], []
    for p in range(moving):
        payload = (packs[p], factor_packs[p])
        by_now = pick(migration_offset, meta[2 + p])
        for level in range((replicas - 1).bit_length()):
            payload = lax.cond(
                jnp.right_shift(by_now, level) % 2 == 1,
                lambda parts, by=1 << level: tuple(shifted(part, "rep", by) for part in parts),
                lambda parts: parts,
                payload,
            )
        caches.append(payload[0])
        factors.append(payload[1])
    return assemble(
        completed,
        [(pack, p, 0, None) for p, pack in enumerate(caches)],
        [(pack, p, 0, None) for p, pack in enumerate(factors)],
    )


def solution(mesh):
    placed = (
        P(("pool", "rep"), "tp"),
        P(("pool", "rep"), "tp"),
        P(("pool", "rep"), "tp"),
        P(("pool", "rep"), "tp"),
        P(("pool", "rep"), None, "tp"),
        P(("pool", "rep"), None, "tp"),
        P("pool"),
        P(("pool", "rep"), "tp", None),
        P(("pool", "rep"), None, "tp"),
        P(("pool", "rep"), None, None, "tp"),
        P("pool", None),
        P(("pool", "rep")),
        P("pool"),
    )
    return jax.shard_map(
        local,
        mesh=mesh,
        in_specs=placed,
        out_specs=(
            P(("pool", "rep"), "tp"),
            P(("pool", "rep"), None, "tp"),
            P(("pool", "rep"), None, "tp"),
            P(("pool", "rep"), "tp", None),
            P(("pool", "rep"), None, "tp"),
            P(("pool", "rep"), None, None, "tp"),
        ),
        check_vma=False,
    )
```

```python
import functools
import itertools
import math

import jax
import jax.numpy as jnp
from jax import lax
from jax.experimental import pallas as pl
from jax.experimental.pallas import tpu as pltpu
from jax.sharding import PartitionSpec as P

HEAD_SIZE = 128
KERNEL_VMEM = 8 << 20


def shifted(shard, axis, by):
    size = lax.axis_size(axis)
    return lax.ppermute(shard, axis, [(i, (i + by) % size) for i in range(size)])


def attend(query, keys, value_rows, key_new, value_new, lengths_now):
    batch_rows = query.shape[0]
    positions = keys.shape[1]
    kv_heads = key_new.shape[1] // HEAD_SIZE
    group_size = query.shape[1] // (kv_heads * HEAD_SIZE)
    factor = 1.0 / math.sqrt(HEAD_SIZE)
    q_heads = query.reshape(batch_rows, kv_heads, group_size, HEAD_SIZE)
    k_heads = keys.reshape(batch_rows, positions, kv_heads, HEAD_SIZE)
    v_heads = value_rows.reshape(batch_rows, positions, kv_heads, HEAD_SIZE)
    new_keys = key_new.reshape(batch_rows, kv_heads, HEAD_SIZE)
    new_values = value_new.reshape(batch_rows, kv_heads, HEAD_SIZE).astype(jnp.float32)
    scores = (
        jnp.einsum("nhgd,nthd->nhgt", q_heads, k_heads, preferred_element_type=jnp.float32) * factor
    )
    fresh = (
        jnp.einsum("nhgd,nhd->nhg", q_heads, new_keys, preferred_element_type=jnp.float32) * factor
    )
    valid = (jnp.arange(positions, dtype=jnp.int32)[None, :] < lengths_now[:, None])[
        :, None, None, :
    ]
    peak = jnp.maximum(jnp.max(jnp.where(valid, scores, -1e30), axis=-1), fresh)
    raised = jnp.where(valid, jnp.exp(scores - peak[..., None]), 0.0)
    raised_new = jnp.exp(fresh - peak)
    total = jnp.sum(raised, axis=-1) + raised_new
    weights = (raised / total[..., None]).astype(jnp.bfloat16)
    weight_new = (raised_new / total).astype(jnp.bfloat16)
    mixed = jnp.einsum("nhgt,nthd->nhgd", weights, v_heads, preferred_element_type=jnp.float32)
    mixed = mixed + weight_new.astype(jnp.float32)[..., None] * new_values[:, :, None, :]
    return mixed.reshape(batch_rows, -1).astype(jnp.bfloat16)


def pick_sum(indicator_matrix, every):
    return jnp.sum(indicator_matrix[:, :, None] * every, axis=1)


def rank_total(partial_rows):
    return lax.psum(partial_rows, "tp").astype(jnp.bfloat16)


def adapter_row_ids(shrunk_part, base_rows, up_factor, indicator_matrix):
    every = jnp.einsum("rk,akc->rac", shrunk_part, up_factor, preferred_element_type=jnp.float32)
    return (base_rows.astype(jnp.float32) + pick_sum(indicator_matrix, every)).astype(jnp.bfloat16)


def adapt_all(
    hidden,
    base_query_proj,
    base_key_proj,
    base_value_proj,
    adapter_down_factors,
    adapter_up_query,
    adapter_up_key_value,
    indicator_matrix,
    rank_extent,
):
    every = jnp.einsum(
        "wb,xbm->wxm", hidden, adapter_down_factors, preferred_element_type=jnp.float32
    )
    shrunk = rank_total(pick_sum(indicator_matrix, every))
    query = adapter_row_ids(
        shrunk[:, :rank_extent], base_query_proj, adapter_up_query, indicator_matrix
    )
    key_new = adapter_row_ids(
        shrunk[:, rank_extent : 2 * rank_extent],
        base_key_proj,
        adapter_up_key_value[:, 0],
        indicator_matrix,
    )
    value_new = adapter_row_ids(
        shrunk[:, 2 * rank_extent :], base_value_proj, adapter_up_key_value[:, 1], indicator_matrix
    )
    return (query, key_new, value_new)


def pick(array, at):
    return lax.dynamic_index_in_dim(array, at, 0, keepdims=False)


def found(values, table):
    at = jnp.int32(0)
    for i, entry in enumerate(table):
        hit = values[0] == entry[0]
        for value, wanted in zip(values[1:], entry[1:]):
            hit = jnp.logical_and(hit, value == wanted)
        at = at + jnp.where(hit, i, 0)
    return at


def gather_kernel(
    table, stay, offset_any, resident_any, ids_any, down_any, upq_any, meta_ref, *rest
):
    packs, (offset_ref, resident_ref, ids_ref, down_ref, upq_ref, sems) = rest[:-6], rest[-6:]
    moving = len(packs)
    loads = [
        pltpu.make_async_copy(source, goal, sems.at[i])
        for i, (source, goal) in enumerate(
            (
                (offset_any, offset_ref),
                (resident_any, resident_ref),
                (ids_any, ids_ref),
                (down_any, down_ref),
                (upq_any, upq_ref),
            )
        )
    ]
    for load in loads:
        load.start()
    for load in loads[:3]:
        load.wait()
    me = lax.axis_index("rep")
    offset = [offset_ref[m] for m in range(moving)]
    place = [
        sum((offset[k] < offset[m]).astype(jnp.int32) for k in range(moving) if k != m)
        for m in range(moving)
    ]
    slot_at = [sum(jnp.where(place[m] == p, m, 0) for m in range(moving)) for p in range(moving)]
    split = down_ref.shape[1]
    pairs = []
    for p in range(moving):
        mine = ids_ref[stay + slot_at[p]]
        loaded = sum(
            jnp.where(resident_ref[n, me] == mine, n, 0) for n in range(resident_ref.shape[0])
        )
        meta_ref[2 + p] = slot_at[p]
        pairs.append((down_ref.at[loaded], packs[p].at[pl.ds(0, split)]))
        pairs.append((upq_ref.at[loaded], packs[p].at[pl.ds(split, upq_ref.shape[1])]))
    copies = [
        pltpu.make_async_copy(src, dst, sems.at[len(loads) + i])
        for i, (src, dst) in enumerate(pairs)
    ]
    for load in loads[3:]:
        load.wait()
    for copy in copies:
        copy.start()
    offset_at = [
        sum(jnp.where(place[m] == p, offset[m], 0) for m in range(moving)) for p in range(moving)
    ]
    meta_ref[0] = found(offset_at, table)
    meta_ref[1] = found(slot_at, list(itertools.permutations(range(moving))))
    for copy in copies:
        copy.wait()


def place_kernel(splits, pieces, row_arrays, stay, meta_ref, *rest):
    packs, rest, sems = rest[: len(pieces)], rest[len(pieces) : -1], rest[-1]
    if row_arrays:
        rows_in, rows_out, rows_now = rest[0], rest[-2], rest[-1]
        rest = rest[1:-2]
    outs = rest[-len(splits) :]
    pool, copies = lax.axis_index("pool"), []
    for pack, (place, first_row, rows, pools) in zip(packs, pieces):
        slot = meta_ref[2 + place]
        start = 0
        for out, wanted in zip(outs, splits):
            first, last = max(start, first_row), min(start + wanted, first_row + rows)
            if first < last:
                copy = pltpu.make_async_copy(
                    pack.at[pl.ds(first - first_row, last - first)],
                    out.at[slot, pl.ds(first - start, last - first)],
                    sems.at[len(copies)],
                )
                copies.append((copy, pools))
            start += wanted

    def in_pools(pools):
        return sum((pool == q).astype(jnp.int32) for q in pools) > 0

    def each(act):
        for copy, pools in copies:
            if pools is None:
                act(copy)
            else:
                pl.when(in_pools(pools))(functools.partial(act, copy))

    each(lambda copy: copy.start())
    if row_arrays:
        now = rows_in[...].astype(jnp.float32)
        at = lax.broadcasted_iota(jnp.int32, now.shape, 0)
        for place, holders in row_arrays:
            row = None
            for i in holders:
                tail = packs[i][pl.ds(packs[i].shape[0] - 16, 16), :].astype(jnp.float32)
                parts = now.shape[1] // tail.shape[1]
                flat = jnp.concatenate([tail[c : c + 1] for c in range(parts)], axis=1)
                row = flat if row is None else jnp.where(in_pools(pieces[i][3]), flat, row)
            now = jnp.where(at == stay + meta_ref[2 + place], row, now)
        rows_now[...] = now.astype(rows_now.dtype)
        leaving = pltpu.make_async_copy(rows_now, rows_out, sems.at[len(copies)])
        leaving.start()
        leaving.wait()
    each(lambda copy: copy.wait())


def place_packs(meta, moving, pieces, splits, attended=None, into=None):
    arrays = [piece[0] for piece in pieces]
    width = arrays[0].shape[1]
    where = tuple((place, first, array.shape[0], pools) for array, place, first, pools in pieces)
    vmem, hbm = (pl.BlockSpec(memory_space=space) for space in (pltpu.VMEM, pltpu.HBM))
    out_shape = [jax.ShapeDtypeStruct((moving, rows, width), arrays[0].dtype) for rows in splits]
    in_specs = [pl.BlockSpec(memory_space=pltpu.SMEM)] + [vmem] * len(arrays)
    scratch = [pltpu.SemaphoreType.DMA((len(pieces) * len(splits) + 1,))]
    row_arrays, stay = None, None
    if attended is not None:
        end = max(first + rows for _, first, rows, _ in where)
        row_arrays = [
            (p, [i for i, (at, first, rows, _) in enumerate(where) if at == p and first + rows == end])
            for p in sorted({place for place, _, _, _ in where})
        ]
        stay = attended.shape[0] - moving
        arrays.append(attended)
        in_specs.append(vmem)
        out_shape.append(jax.ShapeDtypeStruct(attended.shape, attended.dtype))
        scratch.insert(0, pltpu.VMEM(attended.shape, attended.dtype))
    aliases = {}
    if into is not None:
        aliases = {1 + len(arrays) + i: i for i in range(len(splits))}
        arrays = arrays + list(into)
        in_specs = in_specs + [hbm] * len(splits)
    return pl.pallas_call(
        functools.partial(place_kernel, splits, where, row_arrays, stay),
        out_shape=out_shape,
        in_specs=in_specs,
        out_specs=[hbm] * len(out_shape),
        scratch_shapes=scratch,
        input_output_aliases=aliases,
        compiler_params=pltpu.CompilerParams(vmem_limit_bytes=KERNEL_VMEM),
        cost_estimate=pl.CostEstimate(
            flops=0, bytes_accessed=4 * sum(array.size for array in arrays), transcendentals=0
        ),
    )(meta, *arrays)


def joint_kernel(table, meta_ref, other_ref, joint_ref):
    moving = other_ref.shape[0]
    own = meta_ref[0]
    other = jnp.int32(0)
    for i, entry in enumerate(table):
        hits = sum(
            (other_ref[m] == by).astype(jnp.int32) for m in range(moving) for by in entry
        )
        other = other + jnp.where(hits == moving, i, 0)
    size = len(table)
    first = lax.axis_index("pool") == 0
    joint_ref[0] = jnp.where(first, own * size + other, other * size + own)


def distance(shift, replicas):
    return min(shift % replicas, -shift % replicas)


def local(
    hidden,
    base_query_proj,
    base_key_proj,
    base_value_proj,
    key_cache,
    value_cache,
    lengths,
    adapter_down_factors,
    adapter_up_query,
    adapter_up_key_value,
    resident,
    request_adapter_id,
    migration_offset,
):
    count, model_part = hidden.shape
    moving = migration_offset.shape[0]
    stay = count - moving
    rank_extent, query_part = adapter_up_query.shape[1:]
    rank_rows = adapter_down_factors.shape[2]
    positions, kv_width = key_cache.shape[1:]
    replicas = lax.axis_size("rep")
    me = lax.axis_index("rep")
    table = list(itertools.combinations(range(1, replicas), moving))
    pools = lax.axis_size("pool")
    first_hop = (1, -1)
    joint = (
        pools == 2
        and moving == 2
        and len(table) > 0
        and all(
            sum((by[p] - first_hop[p]) % replicas != 0 for p in range(moving)) <= 1
            for by in table
        )
    )

    pack_rows = rank_rows + rank_extent
    cache_rows = 2 * positions + 2 * rank_extent + -(-model_part // (16 * kv_width)) * 16
    row_rows = -(-model_part // (16 * kv_width)) * 16
    small = (migration_offset, resident.T, request_adapter_id)
    factors = (jnp.swapaxes(adapter_down_factors, 1, 2), adapter_up_query)
    meta, *factor_packs = pl.pallas_call(
        functools.partial(gather_kernel, table if joint else [], stay),
        out_shape=[jax.ShapeDtypeStruct((2 + moving,), jnp.int32)]
        + [jax.ShapeDtypeStruct((pack_rows, query_part), hidden.dtype)] * moving,
        in_specs=[pl.BlockSpec(memory_space=pltpu.HBM)] * 5,
        out_specs=[pl.BlockSpec(memory_space=pltpu.SMEM)]
        + [pl.BlockSpec(memory_space=pltpu.HBM)] * moving,
        scratch_shapes=[pltpu.SMEM(array.shape, array.dtype) for array in small]
        + [pltpu.VMEM(array.shape, array.dtype) for array in factors]
        + [pltpu.SemaphoreType.DMA((5 + 2 * moving,))],
        compiler_params=pltpu.CompilerParams(vmem_limit_bytes=KERNEL_VMEM),
        cost_estimate=pl.CostEstimate(
            flops=0, bytes_accessed=4 * moving * pack_rows * query_part, transcendentals=0
        ),
    )(*small, *factors)

    def compute(slots):
        res_row = pick(resident, me)
        indicator_matrix = (request_adapter_id[:, None] == res_row[None, :]).astype(jnp.float32)
        own_lengths = lax.dynamic_slice_in_dim(lengths, me * count, count)
        query, key_new, value_new = adapt_all(
            hidden,
            base_query_proj,
            base_key_proj,
            base_value_proj,
            adapter_down_factors,
            adapter_up_query,
            adapter_up_key_value,
            indicator_matrix,
            rank_extent,
        )
        completed = attend(query, key_cache, value_cache, key_new, value_new, own_lengths)
        packs = []
        for slot in slots:
            row = stay + slot
            at = (jnp.arange(positions, dtype=jnp.int32) == own_lengths[row])[:, None]
            up_pair = sum(
                jnp.where(indicator_matrix[row, n] == 1, adapter_up_key_value[n], 0)
                for n in range(res_row.shape[0])
            )
            packs.append(
                jnp.concatenate(
                    [
                        jnp.where(at, key_new[row][None, :], key_cache[row]),
                        jnp.where(at, value_new[row][None, :], value_cache[row]),
                        up_pair.reshape(-1, kv_width),
                        jnp.pad(
                            completed[row].reshape(-1, kv_width),
                            ((0, row_rows - model_part // kv_width), (0, 0)),
                        ),
                    ]
                )
            )
        return (completed, *packs)

    def compute_now():
        orders = itertools.permutations(range(moving))
        return lax.switch(meta[1], [functools.partial(compute, slots) for slots in orders])

    def assemble(completed, cache_pieces, factor_pieces, last=moving - 1):
        down, upq = place_packs(meta, moving, factor_pieces, (rank_rows, rank_extent))
        cache_parts = (positions, positions, 2 * rank_extent)
        attended, into = completed, None
        for p in [p for p in range(moving) if p != last] + [last]:
            slots, attended, into, (down, upq) = lax.optimization_barrier(
                (meta, attended, into, (down, upq))
            )
            mine = [piece for piece in cache_pieces if piece[1] == p]
            *into, attended = place_packs(slots, moving, mine, cache_parts, attended, into)
        keys, value_rows, up_pair = into
        return (
            attended,
            keys,
            value_rows,
            jnp.swapaxes(down, 1, 2),
            upq,
            up_pair.reshape(moving, 2, rank_extent, kv_width),
        )

    if joint:
        halfway = [shifted(factor_packs[p], "rep", first_hop[p]) for p in range(moving)]
        other_offset = lax.ppermute(migration_offset, "pool", [(0, 1), (1, 0)])
        chosen = pl.pallas_call(
            functools.partial(joint_kernel, table),
            out_shape=jax.ShapeDtypeStruct((1,), jnp.int32),
            in_specs=[pl.BlockSpec(memory_space=pltpu.SMEM)] * 2,
            out_specs=pl.BlockSpec(memory_space=pltpu.SMEM),
            compiler_params=pltpu.CompilerParams(vmem_limit_bytes=KERNEL_VMEM),
        )(meta, other_offset)
        resident, chosen = lax.optimization_barrier((resident, chosen))
        completed, *cache_packs = compute_now()

        def sent(array, routes):
            pairs = [
                (start * replicas + r, end * replicas + (r + shift) % replicas)
                for start, end, shift in routes
                for r in range(replicas)
            ]
            return lax.ppermute(array, ("pool", "rep"), pairs)

        def plan(by):
            left = [[(by[q][p] - first_hop[p]) % replicas for p in range(moving)] for q in (0, 1)]
            loads = [
                sum(
                    distance(by[q][p], replicas) * cache_rows * kv_width
                    + distance(left[q][p], replicas) * pack_rows * query_part
                    for p in range(moving)
                )
                for q in (0, 1)
            ]
            slow = loads.index(max(loads))
            hops = [distance(shift, replicas) for shift in by[slow]]
            far = hops.index(max(hops))
            share = (max(loads) - min(loads)) / (2 * hops[far] * kv_width)
            return left, slow, far, cache_rows - min(int(share) // 16 * 16, cache_rows - 16)

        plans = {by: plan(by) for by in itertools.product(table, repeat=pools)}
        cuts = sorted({(far, kept) for _, _, far, kept in plans.values() if kept < cache_rows})
        pieces_of = {
            (far, kept): (cache_packs[far][:kept], cache_packs[far][kept:]) for far, kept in cuts
        }
        crossed = {}
        for kept in sorted({kept for _, kept in cuts}):
            own = [pieces_of[far, kept][1] for far, size in cuts if size == kept]
            places = [far for far, size in cuts if size == kept]
            part = own[0]
            for place, other in zip(places[1:], own[1:]):
                mine = jnp.bool_(False)
                for i, by in enumerate(table):
                    hops = [distance(shift, replicas) for shift in by]
                    if hops.index(max(hops)) == place:
                        mine = mine | (meta[0] == i)
                part = jnp.where(mine, other, part)
            crossed[kept] = lax.ppermute(part, "pool", [(0, 1), (1, 0)])
        chosen, pieces_of = lax.optimization_barrier((chosen, pieces_of))

        def branch(by):
            left, slow, far, kept = plans[by]
            fast = 1 - slow

            def run():
                factor_pieces, cache_pieces = [], []
                going = {q: p for q in (0, 1) for p in range(moving) if left[q][p] != 0}
                if going:
                    operands = [halfway[going.get(q, going[slow])] for q in (0, 1)]
                    operand = operands[0]
                    if operands[1] is not operand:
                        operand = jnp.where(lax.axis_index("pool") == 0, *operands)
                    hop = sent(operand, [(q, q, left[q][p]) for q, p in going.items()])
                for p in range(moving):
                    there = [q for q in (0, 1) if going.get(q) == p]
                    if there:
                        factor_pieces.append((hop, p, 0, there))
                    stayed = [q for q in (0, 1) if q not in there]
                    if stayed:
                        factor_pieces.append((halfway[p], p, 0, stayed))
                    whole = cache_packs[p]
                    own_way = [(q, q, by[q][p]) for q in (0, 1)]
                    if p == far and kept < cache_rows:
                        direct_part, part = pieces_of[far, kept]
                        cache_pieces.append((sent(direct_part, own_way), p, 0, None))
                        direct = sent(part, [(fast, fast, by[fast][p])])
                        cache_pieces.append((direct, p, kept, [fast]))
                        round_about = sent(crossed[kept], [(fast, slow, by[slow][p])])
                        cache_pieces.append((round_about, p, kept, [slow]))
                    else:
                        cache_pieces.append((sent(whole, own_way), p, 0, None))
                return assemble(completed, cache_pieces, factor_pieces, far)

            return run

        return lax.switch(chosen[0], [branch(by) for by in plans])

    completed, *packs = compute_now()
    caches, factors = [], []
    for p in range(moving):
        payload = (packs[p], factor_packs[p])
        by_now = pick(migration_offset, meta[2 + p])
        for level in range((replicas - 1).bit_length()):
            payload = lax.cond(
                jnp.right_shift(by_now, level) % 2 == 1,
                lambda parts, by=1 << level: tuple(shifted(part, "rep", by) for part in parts),
                lambda parts: parts,
                payload,
            )
        caches.append(payload[0])
        factors.append(payload[1])
    return assemble(
        completed,
        [(pack, p, 0, None) for p, pack in enumerate(caches)],
        [(pack, p, 0, None) for p, pack in enumerate(factors)],
    )


def solution(mesh):
    placed = (
        P(("pool", "rep"), "tp"),
        P(("pool", "rep"), "tp"),
        P(("pool", "rep"), "tp"),
        P(("pool", "rep"), "tp"),
        P(("pool", "rep"), None, "tp"),
        P(("pool", "rep"), None, "tp"),
        P("pool"),
        P(("pool", "rep"), "tp", None),
        P(("pool", "rep"), None, "tp"),
        P(("pool", "rep"), None, None, "tp"),
        P("pool", None),
        P(("pool", "rep")),
        P("pool"),
    )
    return jax.shard_map(
        local,
        mesh=mesh,
        in_specs=placed,
        out_specs=(
            P(("pool", "rep"), "tp"),
            P(("pool", "rep"), None, "tp"),
            P(("pool", "rep"), None, "tp"),
            P(("pool", "rep"), "tp", None),
            P(("pool", "rep"), None, "tp"),
            P(("pool", "rep"), None, None, "tp"),
        ),
        check_vma=False,
    )
```

```python
import functools
import itertools
import math

import jax
import jax.numpy as jnp
from jax import lax
from jax.experimental import pallas as pl
from jax.experimental.pallas import tpu as pltpu
from jax.sharding import PartitionSpec as P

HEAD_SIZE = 128
KERNEL_VMEM = 8 << 20
RELAY_BIAS = 1.06


def shifted(shard, axis, by):
    size = lax.axis_size(axis)
    return lax.ppermute(shard, axis, [(i, (i + by) % size) for i in range(size)])


def attend(query, keys, value_rows, key_new, value_new, lengths_now):
    batch_rows = query.shape[0]
    positions = keys.shape[1]
    kv_heads = key_new.shape[1] // HEAD_SIZE
    group_size = query.shape[1] // (kv_heads * HEAD_SIZE)
    factor = 1.0 / math.sqrt(HEAD_SIZE)
    q_heads = query.reshape(batch_rows, kv_heads, group_size, HEAD_SIZE)
    k_heads = keys.reshape(batch_rows, positions, kv_heads, HEAD_SIZE)
    v_heads = value_rows.reshape(batch_rows, positions, kv_heads, HEAD_SIZE)
    new_keys = key_new.reshape(batch_rows, kv_heads, HEAD_SIZE)
    new_values = value_new.reshape(batch_rows, kv_heads, HEAD_SIZE).astype(jnp.float32)
    scores = (
        jnp.einsum("nhgd,nthd->nhgt", q_heads, k_heads, preferred_element_type=jnp.float32) * factor
    )
    fresh = (
        jnp.einsum("nhgd,nhd->nhg", q_heads, new_keys, preferred_element_type=jnp.float32) * factor
    )
    valid = (jnp.arange(positions, dtype=jnp.int32)[None, :] < lengths_now[:, None])[
        :, None, None, :
    ]
    peak = jnp.maximum(jnp.max(jnp.where(valid, scores, -1e30), axis=-1), fresh)
    raised = jnp.where(valid, jnp.exp(scores - peak[..., None]), 0.0)
    raised_new = jnp.exp(fresh - peak)
    total = jnp.sum(raised, axis=-1) + raised_new
    weights = (raised / total[..., None]).astype(jnp.bfloat16)
    weight_new = (raised_new / total).astype(jnp.bfloat16)
    mixed = jnp.einsum("nhgt,nthd->nhgd", weights, v_heads, preferred_element_type=jnp.float32)
    mixed = mixed + weight_new.astype(jnp.float32)[..., None] * new_values[:, :, None, :]
    return mixed.reshape(batch_rows, -1).astype(jnp.bfloat16)


def pick_sum(indicator_matrix, every):
    return jnp.sum(indicator_matrix[:, :, None] * every, axis=1)


def rank_total(partial_rows):
    return lax.psum(partial_rows, "tp").astype(jnp.bfloat16)


def adapter_row_ids(shrunk_part, base_rows, up_factor, indicator_matrix):
    every = jnp.einsum("rk,akc->rac", shrunk_part, up_factor, preferred_element_type=jnp.float32)
    return (base_rows.astype(jnp.float32) + pick_sum(indicator_matrix, every)).astype(jnp.bfloat16)


def adapt_all(
    hidden,
    base_query_proj,
    base_key_proj,
    base_value_proj,
    adapter_down_factors,
    adapter_up_query,
    adapter_up_key_value,
    indicator_matrix,
    rank_extent,
):
    every = jnp.einsum(
        "wb,xbm->wxm", hidden, adapter_down_factors, preferred_element_type=jnp.float32
    )
    shrunk = rank_total(pick_sum(indicator_matrix, every))
    query = adapter_row_ids(
        shrunk[:, :rank_extent], base_query_proj, adapter_up_query, indicator_matrix
    )
    key_new = adapter_row_ids(
        shrunk[:, rank_extent : 2 * rank_extent],
        base_key_proj,
        adapter_up_key_value[:, 0],
        indicator_matrix,
    )
    value_new = adapter_row_ids(
        shrunk[:, 2 * rank_extent :], base_value_proj, adapter_up_key_value[:, 1], indicator_matrix
    )
    return (query, key_new, value_new)


def pick(array, at):
    return lax.dynamic_index_in_dim(array, at, 0, keepdims=False)


def found(values, table):
    at = jnp.int32(0)
    for i, entry in enumerate(table):
        hit = values[0] == entry[0]
        for value, wanted in zip(values[1:], entry[1:]):
            hit = jnp.logical_and(hit, value == wanted)
        at = at + jnp.where(hit, i, 0)
    return at


def gather_kernel(
    table, stay, offset_any, resident_any, ids_any, down_any, upq_any, meta_ref, *rest
):
    packs, (offset_ref, resident_ref, ids_ref, down_ref, upq_ref, sems) = rest[:-6], rest[-6:]
    moving = len(packs)
    loads = [
        pltpu.make_async_copy(source, goal, sems.at[i])
        for i, (source, goal) in enumerate(
            (
                (offset_any, offset_ref),
                (resident_any, resident_ref),
                (ids_any, ids_ref),
                (down_any, down_ref),
                (upq_any, upq_ref),
            )
        )
    ]
    for load in loads:
        load.start()
    for load in loads[:3]:
        load.wait()
    me = lax.axis_index("rep")
    offset = [offset_ref[m] for m in range(moving)]
    place = [
        sum((offset[k] < offset[m]).astype(jnp.int32) for k in range(moving) if k != m)
        for m in range(moving)
    ]
    slot_at = [sum(jnp.where(place[m] == p, m, 0) for m in range(moving)) for p in range(moving)]
    split = down_ref.shape[1]
    pairs = []
    for p in range(moving):
        mine = ids_ref[stay + slot_at[p]]
        loaded = sum(
            jnp.where(resident_ref[n, me] == mine, n, 0) for n in range(resident_ref.shape[0])
        )
        meta_ref[2 + p] = slot_at[p]
        pairs.append((down_ref.at[loaded], packs[p].at[pl.ds(0, split)]))
        pairs.append((upq_ref.at[loaded], packs[p].at[pl.ds(split, upq_ref.shape[1])]))
    copies = [
        pltpu.make_async_copy(src, dst, sems.at[len(loads) + i])
        for i, (src, dst) in enumerate(pairs)
    ]
    for load in loads[3:]:
        load.wait()
    for copy in copies:
        copy.start()
    offset_at = [
        sum(jnp.where(place[m] == p, offset[m], 0) for m in range(moving)) for p in range(moving)
    ]
    meta_ref[0] = found(offset_at, table)
    meta_ref[1] = found(slot_at, list(itertools.permutations(range(moving))))
    for copy in copies:
        copy.wait()


def place_kernel(splits, pieces, row_arrays, stay, meta_ref, *rest):
    packs, rest, sems = rest[: len(pieces)], rest[len(pieces) : -1], rest[-1]
    if row_arrays:
        rows_in, rows_out, rows_now = rest[0], rest[-2], rest[-1]
        rest = rest[1:-2]
    outs = rest[-len(splits) :]
    pool, copies = lax.axis_index("pool"), []
    for pack, (place, first_row, rows, pools) in zip(packs, pieces):
        slot = meta_ref[2 + place]
        start = 0
        for out, wanted in zip(outs, splits):
            first, last = max(start, first_row), min(start + wanted, first_row + rows)
            if first < last:
                copy = pltpu.make_async_copy(
                    pack.at[pl.ds(first - first_row, last - first)],
                    out.at[slot, pl.ds(first - start, last - first)],
                    sems.at[len(copies)],
                )
                copies.append((copy, pools))
            start += wanted

    def in_pools(pools):
        return sum((pool == q).astype(jnp.int32) for q in pools) > 0

    def each(act):
        for copy, pools in copies:
            if pools is None:
                act(copy)
            else:
                pl.when(in_pools(pools))(functools.partial(act, copy))

    each(lambda copy: copy.start())
    if row_arrays:
        now = rows_in[...].astype(jnp.float32)
        at = lax.broadcasted_iota(jnp.int32, now.shape, 0)
        for place, holders in row_arrays:
            row = None
            for i in holders:
                tail = packs[i][pl.ds(packs[i].shape[0] - 16, 16), :].astype(jnp.float32)
                parts = now.shape[1] // tail.shape[1]
                flat = jnp.concatenate([tail[c : c + 1] for c in range(parts)], axis=1)
                row = flat if row is None else jnp.where(in_pools(pieces[i][3]), flat, row)
            now = jnp.where(at == stay + meta_ref[2 + place], row, now)
        rows_now[...] = now.astype(rows_now.dtype)
        leaving = pltpu.make_async_copy(rows_now, rows_out, sems.at[len(copies)])
        leaving.start()
        leaving.wait()
    each(lambda copy: copy.wait())


def place_packs(meta, moving, pieces, splits, attended=None, into=None):
    arrays = [piece[0] for piece in pieces]
    width = arrays[0].shape[1]
    where = tuple((place, first, array.shape[0], pools) for array, place, first, pools in pieces)
    vmem, hbm = (pl.BlockSpec(memory_space=space) for space in (pltpu.VMEM, pltpu.HBM))
    out_shape = [jax.ShapeDtypeStruct((moving, rows, width), arrays[0].dtype) for rows in splits]
    in_specs = [pl.BlockSpec(memory_space=pltpu.SMEM)] + [vmem] * len(arrays)
    scratch = [pltpu.SemaphoreType.DMA((len(pieces) * len(splits) + 1,))]
    row_arrays, stay = None, None
    if attended is not None:
        end = max(first + rows for _, first, rows, _ in where)
        row_arrays = [
            (p, [i for i, (at, first, rows, _) in enumerate(where) if at == p and first + rows == end])
            for p in sorted({place for place, _, _, _ in where})
        ]
        stay = attended.shape[0] - moving
        arrays.append(attended)
        in_specs.append(vmem)
        out_shape.append(jax.ShapeDtypeStruct(attended.shape, attended.dtype))
        scratch.insert(0, pltpu.VMEM(attended.shape, attended.dtype))
    aliases = {}
    if into is not None:
        aliases = {1 + len(arrays) + i: i for i in range(len(splits))}
        arrays = arrays + list(into)
        in_specs = in_specs + [hbm] * len(splits)
    return pl.pallas_call(
        functools.partial(place_kernel, splits, where, row_arrays, stay),
        out_shape=out_shape,
        in_specs=in_specs,
        out_specs=[hbm] * len(out_shape),
        scratch_shapes=scratch,
        input_output_aliases=aliases,
        compiler_params=pltpu.CompilerParams(vmem_limit_bytes=KERNEL_VMEM),
        cost_estimate=pl.CostEstimate(
            flops=0, bytes_accessed=4 * sum(array.size for array in arrays), transcendentals=0
        ),
    )(meta, *arrays)


def joint_kernel(table, meta_ref, other_ref, joint_ref):
    moving = other_ref.shape[0]
    own = meta_ref[0]
    other = jnp.int32(0)
    for i, entry in enumerate(table):
        hits = sum(
            (other_ref[m] == by).astype(jnp.int32) for m in range(moving) for by in entry
        )
        other = other + jnp.where(hits == moving, i, 0)
    size = len(table)
    first = lax.axis_index("pool") == 0
    joint_ref[0] = jnp.where(first, own * size + other, other * size + own)


def distance(shift, replicas):
    return min(shift % replicas, -shift % replicas)


def local(
    hidden,
    base_query_proj,
    base_key_proj,
    base_value_proj,
    key_cache,
    value_cache,
    lengths,
    adapter_down_factors,
    adapter_up_query,
    adapter_up_key_value,
    resident,
    request_adapter_id,
    migration_offset,
):
    count, model_part = hidden.shape
    moving = migration_offset.shape[0]
    stay = count - moving
    rank_extent, query_part = adapter_up_query.shape[1:]
    rank_rows = adapter_down_factors.shape[2]
    positions, kv_width = key_cache.shape[1:]
    replicas = lax.axis_size("rep")
    me = lax.axis_index("rep")
    table = list(itertools.combinations(range(1, replicas), moving))
    pools = lax.axis_size("pool")
    first_hop = (1, -1)
    joint = (
        pools == 2
        and moving == 2
        and len(table) > 0
        and all(
            sum((by[p] - first_hop[p]) % replicas != 0 for p in range(moving)) <= 1
            for by in table
        )
    )

    pack_rows = rank_rows + rank_extent
    cache_rows = 2 * positions + 2 * rank_extent + -(-model_part // (16 * kv_width)) * 16
    row_rows = -(-model_part // (16 * kv_width)) * 16
    small = (migration_offset, resident.T, request_adapter_id)
    factors = (jnp.swapaxes(adapter_down_factors, 1, 2), adapter_up_query)
    meta, *factor_packs = pl.pallas_call(
        functools.partial(gather_kernel, table if joint else [], stay),
        out_shape=[jax.ShapeDtypeStruct((2 + moving,), jnp.int32)]
        + [jax.ShapeDtypeStruct((pack_rows, query_part), hidden.dtype)] * moving,
        in_specs=[pl.BlockSpec(memory_space=pltpu.HBM)] * 5,
        out_specs=[pl.BlockSpec(memory_space=pltpu.SMEM)]
        + [pl.BlockSpec(memory_space=pltpu.HBM)] * moving,
        scratch_shapes=[pltpu.SMEM(array.shape, array.dtype) for array in small]
        + [pltpu.VMEM(array.shape, array.dtype) for array in factors]
        + [pltpu.SemaphoreType.DMA((5 + 2 * moving,))],
        compiler_params=pltpu.CompilerParams(vmem_limit_bytes=KERNEL_VMEM),
        cost_estimate=pl.CostEstimate(
            flops=0, bytes_accessed=4 * moving * pack_rows * query_part, transcendentals=0
        ),
    )(*small, *factors)

    def compute(slots):
        res_row = pick(resident, me)
        indicator_matrix = (request_adapter_id[:, None] == res_row[None, :]).astype(jnp.float32)
        own_lengths = lax.dynamic_slice_in_dim(lengths, me * count, count)
        query, key_new, value_new = adapt_all(
            hidden,
            base_query_proj,
            base_key_proj,
            base_value_proj,
            adapter_down_factors,
            adapter_up_query,
            adapter_up_key_value,
            indicator_matrix,
            rank_extent,
        )
        completed = attend(query, key_cache, value_cache, key_new, value_new, own_lengths)
        packs = []
        for slot in slots:
            row = stay + slot
            at = (jnp.arange(positions, dtype=jnp.int32) == own_lengths[row])[:, None]
            up_pair = sum(
                jnp.where(indicator_matrix[row, n] == 1, adapter_up_key_value[n], 0)
                for n in range(res_row.shape[0])
            )
            packs.append(
                jnp.concatenate(
                    [
                        jnp.where(at, key_new[row][None, :], key_cache[row]),
                        jnp.where(at, value_new[row][None, :], value_cache[row]),
                        up_pair.reshape(-1, kv_width),
                        jnp.pad(
                            completed[row].reshape(-1, kv_width),
                            ((0, row_rows - model_part // kv_width), (0, 0)),
                        ),
                    ]
                )
            )
        return (completed, *packs)

    def compute_now():
        orders = itertools.permutations(range(moving))
        return lax.switch(meta[1], [functools.partial(compute, slots) for slots in orders])

    def assemble(completed, cache_pieces, factor_pieces, last=moving - 1):
        down, upq = place_packs(meta, moving, factor_pieces, (rank_rows, rank_extent))
        cache_parts = (positions, positions, 2 * rank_extent)
        attended, into = completed, None
        for p in [p for p in range(moving) if p != last] + [last]:
            slots, attended, into, (down, upq) = lax.optimization_barrier(
                (meta, attended, into, (down, upq))
            )
            mine = [piece for piece in cache_pieces if piece[1] == p]
            *into, attended = place_packs(slots, moving, mine, cache_parts, attended, into)
        keys, value_rows, up_pair = into
        return (
            attended,
            keys,
            value_rows,
            jnp.swapaxes(down, 1, 2),
            upq,
            up_pair.reshape(moving, 2, rank_extent, kv_width),
        )

    if joint:
        halfway = [shifted(factor_packs[p], "rep", first_hop[p]) for p in range(moving)]
        other_offset = lax.ppermute(migration_offset, "pool", [(0, 1), (1, 0)])
        chosen = pl.pallas_call(
            functools.partial(joint_kernel, table),
            out_shape=jax.ShapeDtypeStruct((1,), jnp.int32),
            in_specs=[pl.BlockSpec(memory_space=pltpu.SMEM)] * 2,
            out_specs=pl.BlockSpec(memory_space=pltpu.SMEM),
            compiler_params=pltpu.CompilerParams(vmem_limit_bytes=KERNEL_VMEM),
        )(meta, other_offset)
        resident, chosen = lax.optimization_barrier((resident, chosen))
        completed, *cache_packs = compute_now()

        def sent(array, routes):
            pairs = [
                (start * replicas + r, end * replicas + (r + shift) % replicas)
                for start, end, shift in routes
                for r in range(replicas)
            ]
            return lax.ppermute(array, ("pool", "rep"), pairs)

        def plan(by):
            left = [[(by[q][p] - first_hop[p]) % replicas for p in range(moving)] for q in (0, 1)]
            loads = [
                sum(
                    distance(by[q][p], replicas) * cache_rows * kv_width
                    + distance(left[q][p], replicas) * pack_rows * query_part
                    for p in range(moving)
                )
                for q in (0, 1)
            ]
            slow = loads.index(max(loads))
            hops = [distance(shift, replicas) for shift in by[slow]]
            far = hops.index(max(hops))
            share = RELAY_BIAS * (max(loads) - min(loads)) / (2 * hops[far] * kv_width)
            return left, slow, far, cache_rows - min(int(share) // 16 * 16, cache_rows - 16)

        plans = {by: plan(by) for by in itertools.product(table, repeat=pools)}
        cuts = sorted({(far, kept) for _, _, far, kept in plans.values() if kept < cache_rows})
        pieces_of = {
            (far, kept): (cache_packs[far][:kept], cache_packs[far][kept:]) for far, kept in cuts
        }
        crossed = {}
        for kept in sorted({kept for _, kept in cuts}):
            own = [pieces_of[far, kept][1] for far, size in cuts if size == kept]
            places = [far for far, size in cuts if size == kept]
            part = own[0]
            for place, other in zip(places[1:], own[1:]):
                mine = jnp.bool_(False)
                for i, by in enumerate(table):
                    hops = [distance(shift, replicas) for shift in by]
                    if hops.index(max(hops)) == place:
                        mine = mine | (meta[0] == i)
                part = jnp.where(mine, other, part)
            crossed[kept] = lax.ppermute(part, "pool", [(0, 1), (1, 0)])
        chosen, pieces_of = lax.optimization_barrier((chosen, pieces_of))

        def branch(by):
            left, slow, far, kept = plans[by]
            fast = 1 - slow

            def run():
                factor_pieces, cache_pieces = [], []
                going = {q: p for q in (0, 1) for p in range(moving) if left[q][p] != 0}
                if going:
                    operands = [halfway[going.get(q, going[slow])] for q in (0, 1)]
                    operand = operands[0]
                    if operands[1] is not operand:
                        operand = jnp.where(lax.axis_index("pool") == 0, *operands)
                    hop = sent(operand, [(q, q, left[q][p]) for q, p in going.items()])
                for p in range(moving):
                    there = [q for q in (0, 1) if going.get(q) == p]
                    if there:
                        factor_pieces.append((hop, p, 0, there))
                    stayed = [q for q in (0, 1) if q not in there]
                    if stayed:
                        factor_pieces.append((halfway[p], p, 0, stayed))
                    whole = cache_packs[p]
                    own_way = [(q, q, by[q][p]) for q in (0, 1)]
                    if p == far and kept < cache_rows:
                        direct_part, part = pieces_of[far, kept]
                        cache_pieces.append((sent(direct_part, own_way), p, 0, None))
                        direct = sent(part, [(fast, fast, by[fast][p])])
                        cache_pieces.append((direct, p, kept, [fast]))
                        round_about = sent(crossed[kept], [(fast, slow, by[slow][p])])
                        cache_pieces.append((round_about, p, kept, [slow]))
                    else:
                        cache_pieces.append((sent(whole, own_way), p, 0, None))
                return assemble(completed, cache_pieces, factor_pieces, far)

            return run

        return lax.switch(chosen[0], [branch(by) for by in plans])

    completed, *packs = compute_now()
    caches, factors = [], []
    for p in range(moving):
        payload = (packs[p], factor_packs[p])
        by_now = pick(migration_offset, meta[2 + p])
        for level in range((replicas - 1).bit_length()):
            payload = lax.cond(
                jnp.right_shift(by_now, level) % 2 == 1,
                lambda parts, by=1 << level: tuple(shifted(part, "rep", by) for part in parts),
                lambda parts: parts,
                payload,
            )
        caches.append(payload[0])
        factors.append(payload[1])
    return assemble(
        completed,
        [(pack, p, 0, None) for p, pack in enumerate(caches)],
        [(pack, p, 0, None) for p, pack in enumerate(factors)],
    )


def solution(mesh):
    placed = (
        P(("pool", "rep"), "tp"),
        P(("pool", "rep"), "tp"),
        P(("pool", "rep"), "tp"),
        P(("pool", "rep"), "tp"),
        P(("pool", "rep"), None, "tp"),
        P(("pool", "rep"), None, "tp"),
        P("pool"),
        P(("pool", "rep"), "tp", None),
        P(("pool", "rep"), None, "tp"),
        P(("pool", "rep"), None, None, "tp"),
        P("pool", None),
        P(("pool", "rep")),
        P("pool"),
    )
    return jax.shard_map(
        local,
        mesh=mesh,
        in_specs=placed,
        out_specs=(
            P(("pool", "rep"), "tp"),
            P(("pool", "rep"), None, "tp"),
            P(("pool", "rep"), None, "tp"),
            P(("pool", "rep"), "tp", None),
            P(("pool", "rep"), None, "tp"),
            P(("pool", "rep"), None, None, "tp"),
        ),
        check_vma=False,
    )
```
